32 devices in a mesh: dp: 4 (over z), ctx: 8 (over y, x, core).
Axes of the slice: x: 2, y: 2, z: 4, core: 2. Of those that a mesh axis runs over, the one named last changes fastest.
Arguments:
- patches: bfloat16 [8192, 1280], P(('dp', 'ctx')), may hold values from -6 to 6
- unit_counts: int32 [8, 4], P('ctx'), may hold values from 1 to 8, 16 in all within a row
- segment_ids: int32 [4096], P(('dp', 'ctx')), may hold values from 0 to 7, as said below
- merged_position: int32 [1024], P(('dp', 'ctx')), may hold values from 0 to 511, as said below
- ln_gain: float32 [1280], replicated, may hold values from 0.5 to 1.5
- ln_bias: float32 [1280], replicated, may hold values from -3 to 3
- qkv_weight: bfloat16 [1280, 2880], replicated, may hold values from -1 to 1
- out_weight: bfloat16 [960, 1280], replicated, may hold values from -0.1875 to 0.1875
- merge_gain: float32 [1280], replicated, may hold values from 0.5 to 1.5
- merge_bias: float32 [1280], replicated, may hold values from -3 to 3
- merged_grad: bfloat16 [2048, 5120], P(('dp', 'ctx')), may hold values from -6 to 6
Outputs:
- merged: bfloat16 [2048, 5120], P(('dp', 'ctx'))
- patch_grad: bfloat16 [8192, 1280], P(('dp', 'ctx'))
- norm_grads: float32 [4, 1280], replicated
The draws below stay inside these ranges and needn't reach their ends.
Inputs may be any that keep to these rules, and one draw needn't show every extreme that they name: Each row of unit_counts sums to 16; the largest entry of a row is exactly 8. `segment_ids`: constant over each aligned run of 4 rows; 0 at the first row of every block of 32 rows and never falling within a block. `merged_position`: the tokens of device (d, c) have positions in c * 64 to c * 64 + 63, strictly rising along the device's tokens and rising by one within an image.
All inputs are finite; a program needn't handle non-finite values.
Results may differ from the reference program's by a relative error of at most 0.0068.
Values may be sent and summed in bfloat16 or wider, within the bound.
No kernel may reach another device: no remote copies, remote signals or barrier semaphores. Data moves between devices by JAX's collectives and lax.ppermute only.
A program may use at most 64 MiB of HBM per device.

```python
import math
import jax
import jax.numpy as jnp
import numpy as np
from jax import lax

D = 1280
HEAD = 80
HEADS = 12
UNIT = 32
UNITS_DEV = 4
ATT = 960
MERGED = 5120
ROWS = 128
SRC_UNITS = 8
SRC_ROWS = 256
GROUPS = 32
SEQ_DEV = 64
N_DP = 4
N_CTX = 8


def image_layout(key):
    key = jax.random.fold_in(key, 23)
    devices = N_DP * N_CTX
    groups = UNITS_DEV * UNIT // 4
    per_unit = UNIT // 4
    index = jnp.arange(groups, dtype=jnp.int32)
    device_index = jnp.arange(devices, dtype=jnp.int32)
    breaks = jax.random.randint(jax.random.fold_in(key, 1), (devices, groups), 0, 2) == 1
    first = index % per_unit == 0
    forced = (device_index[:, None] == 0) & (index[None, :] < per_unit)
    starts = breaks | first[None, :] | forced
    counted = jnp.cumsum(starts.astype(jnp.int32), axis=1).astype(jnp.int32)
    by_unit = counted.reshape(devices, UNITS_DEV, per_unit)
    image = (by_unit - by_unit[:, :, :1]).reshape(devices, groups)
    gaps = jax.random.randint(jax.random.fold_in(key, 2), (devices, groups), 0, 2) * starts.astype(jnp.int32)
    gaps = gaps.at[:, 0].set(0)
    offset = index[None, :] + jnp.cumsum(gaps, axis=1).astype(jnp.int32)
    column = device_index % N_CTX
    row_rank = device_index // N_CTX
    coin = jax.random.randint(jax.random.fold_in(key, 3), (devices,), 0, 2) == 1
    push = coin & (device_index != 0) | (column == N_CTX - 1) & (row_rank == 0)
    shift = jnp.where(push, 2 * groups - 1 - offset[:, -1], 0)
    offset = offset + shift[:, None]
    position = offset + (column * 2 * groups)[:, None]
    return (image.astype(jnp.int32), position.astype(jnp.int32))


def draw_segment_ids(key, part):
    image, position = image_layout(key)
    return jnp.repeat(image, 4, axis=1).reshape(-1).astype(jnp.int32)


def draw_merged_position(key, part):
    image, position = image_layout(key)
    return position.reshape(-1).astype(jnp.int32)


def draw_qkv_weight(key, part):
    inner = HEADS * HEAD
    base = jax.random.normal(jax.random.fold_in(key, 11), (D, 3 * inner), jnp.float32)
    base = jnp.clip(base, -4.0, 4.0) * D ** (-0.5)
    return base.astype(jnp.bfloat16)


def block_levels(own_key, shape, cuts, least, largest):
    def one(dim, parts):
        draws = jax.random.uniform(jax.random.fold_in(jax.random.fold_in(own_key, 6), dim), (parts,), jnp.float32, least / len(cuts), largest / len(cuts))
        return jnp.repeat(jnp.exp(draws), shape[dim] // parts).reshape((-1,) + (1,) * (len(shape) - dim - 1))

    factor_of = one(*cuts[0])
    for cut in cuts[1:]:
        factor_of = factor_of * one(*cut)
    return factor_of


def length_profile(amount, total, limit, skew):
    loads = [(1 << 20) // math.isqrt(standing ** skew) + 1 for standing in range(2, amount + 1)]
    rest, holding = total - limit - (amount - 1), [1] * (amount - 1)
    while rest > 0:
        candidates = [i for i in range(amount - 1) if holding[i] < limit]
        mass, budget = sum([loads[i] for i in candidates]), rest
        for i in candidates:
            extra = min(limit - holding[i], max(1, budget * loads[i] // mass), rest)
            holding[i] = holding[i] + extra
            rest = rest - extra
    return np.array([limit] + holding)


def uneven(key, count, total, limit, skew):
    if count == 2:
        one = jax.random.randint(key, (), max(1, total - limit), min(limit, total - 1) + 1)
        return jnp.stack([one, total - one])
    tallies = jnp.asarray(length_profile(count, total, limit, skew), jnp.int32)
    pairs = (count - 1) // 2
    source_of, sink = tallies[1:1 + 2 * pairs:2], tallies[2:2 + 2 * pairs:2]
    room = jnp.minimum(source_of - 1, limit - sink)
    moved = jax.random.randint(jax.random.fold_in(key, 1), (pairs,), 0, 1 << 20) % (room + 1)
    tallies = tallies.at[1:1 + 2 * pairs:2].set(source_of - moved).at[2:2 + 2 * pairs:2].set(sink + moved)
    return tallies[jax.random.permutation(jax.random.fold_in(key, 2), count)]


def noise(key, extent, deviation, most, shards=(), held_as=jnp.bfloat16):
    entries = deviation * jax.random.normal(key, extent, jnp.float32)
    if shards:
        entries = entries * block_levels(key, extent, shards, -0.22, 0.18)
    return jnp.clip(entries, -most, most).astype(held_as)


def setup_inputs(seed: int = 0) -> dict:
    streams_of = jax.random.split(jax.random.key(seed), 12)
    return {
        "patches": noise(streams_of[0], (N_DP * N_CTX * SRC_ROWS, D), 1.0, 6.0, ((0, 32),)),
        "unit_counts": jax.vmap(lambda own: uneven(own, N_DP, UNITS_DEV * N_DP, 2 * UNITS_DEV, 2))(jax.random.split(streams_of[1], N_CTX)).reshape((N_CTX, N_DP)).astype(jnp.int32),
        "segment_ids": draw_segment_ids(jax.random.fold_in(streams_of[11], 71), 0),
        "merged_position": draw_merged_position(jax.random.fold_in(streams_of[11], 71), 0),
        "ln_gain": jnp.clip(1.0 + 0.1 * jax.random.normal(streams_of[4], (D,), jnp.float32), 0.5, 1.5),
        "ln_bias": noise(streams_of[5], (D,), 0.5, 3.0, (), jnp.float32),
        "qkv_weight": draw_qkv_weight(jax.random.fold_in(streams_of[11], 71), 0),
        "out_weight": noise(streams_of[7], (ATT, D), ATT ** -0.5, 0.1875),
        "merge_gain": jnp.clip(1.0 + 0.1 * jax.random.normal(streams_of[8], (D,), jnp.float32), 0.5, 1.5),
        "merge_bias": noise(streams_of[9], (D,), 0.5, 3.0, (), jnp.float32),
        "merged_grad": noise(streams_of[10], (N_DP * N_CTX * SEQ_DEV, MERGED), 1.0, 6.0, ((0, 32),)),
    }


EPS = 1e-06
NEG = -1e+30

def norm_parts(values, scale_gain, shift_bias):
    average = lax.optimization_barrier(jnp.mean(values, axis=-1, keepdims=True))
    centred = values - average
    inverse = lax.rsqrt(lax.optimization_barrier(jnp.mean(centred * centred, axis=-1, keepdims=True)) + EPS)
    normed = centred * inverse
    return (normed, inverse, normed * scale_gain + shift_bias)

def norm_back(upstream, normed, inverse, scale_gain):
    scaled = upstream * scale_gain
    centre = lax.optimization_barrier(jnp.mean(scaled, axis=-1, keepdims=True))
    slope = lax.optimization_barrier(jnp.mean(scaled * normed, axis=-1, keepdims=True))
    return inverse * (scaled - centre - normed * slope)

def image_mask(labels):
    length = labels.shape[-1]
    block_of = jnp.arange(length, dtype=jnp.int32) // UNIT
    joined = labels + block_of * UNIT
    return joined[..., :, None] == joined[..., None, :]

def block_forward(rows, labels, ln_gain, ln_bias, qkv_weight, out_weight, merge_gain, merge_bias):
    batch, length, width = rows.shape
    inner = out_weight.shape[0]
    heads = inner // HEAD
    scale = HEAD ** (-0.5)
    flat = rows.reshape(batch * length, width).astype(jnp.float32)
    normed_in, inverse_in, shifted = norm_parts(flat, ln_gain, ln_bias)
    qkv = jnp.dot(shifted.astype(jnp.bfloat16), qkv_weight, preferred_element_type=jnp.float32).astype(jnp.bfloat16)
    split = qkv.reshape(batch, length, 3, heads, HEAD)
    queries = split[:, :, 0]
    key_heads = split[:, :, 1]
    value_heads = split[:, :, 2]
    scores = jnp.einsum('nqhe,nkhe->nhqk', queries.astype(jnp.float32), key_heads.astype(jnp.float32)) * scale
    scores = jnp.where(image_mask(labels)[:, None], scores, NEG)
    peak = lax.optimization_barrier(jnp.max(scores, axis=-1, keepdims=True))
    raised = jnp.exp(scores - peak)
    attention = raised / lax.optimization_barrier(jnp.sum(raised, axis=-1, keepdims=True))
    attention_half = attention.astype(jnp.bfloat16)
    attended = jnp.einsum('nhqk,nkhe->nqhe', attention_half.astype(jnp.float32), value_heads.astype(jnp.float32)).astype(jnp.bfloat16)
    hidden = flat + jnp.dot(attended.reshape(batch * length, inner), out_weight, preferred_element_type=jnp.float32)
    normed_out, inverse_out, result = norm_parts(hidden, merge_gain, merge_bias)
    saved = (normed_in, inverse_in, queries, key_heads, value_heads, attention, attention_half, normed_out, inverse_out)
    return (result.astype(jnp.bfloat16), saved)

def block_backward(upstream, saved, ln_gain, qkv_weight, out_weight, merge_gain):
    normed_in, inverse_in, queries, key_heads, value_heads, attention, attention_half, normed_out, inverse_out = saved
    batch = queries.shape[0]
    length = queries.shape[1]
    heads = queries.shape[2]
    inner = out_weight.shape[0]
    scale = HEAD ** (-0.5)
    merge_scale = lax.optimization_barrier(jnp.sum(upstream * normed_out, axis=0))
    merge_shift = lax.optimization_barrier(jnp.sum(upstream, axis=0))
    hidden_grad = norm_back(upstream, normed_out, inverse_out, merge_gain)
    attended_grad = jnp.dot(hidden_grad.astype(jnp.bfloat16), out_weight.T, preferred_element_type=jnp.float32).astype(jnp.bfloat16)
    attended_grad = attended_grad.reshape(batch, length, heads, HEAD).astype(jnp.float32)
    softmax_grad = jnp.einsum('nqhe,nkhe->nhqk', attended_grad, value_heads.astype(jnp.float32))
    value_grad = jnp.einsum('nhqk,nqhe->nkhe', attention_half.astype(jnp.float32), attended_grad)
    centred = softmax_grad - lax.optimization_barrier(jnp.sum(attention * softmax_grad, axis=-1, keepdims=True))
    score_grad = (attention * centred * scale).astype(jnp.bfloat16).astype(jnp.float32)
    query_grad = jnp.einsum('nhqk,nkhe->nqhe', score_grad, key_heads.astype(jnp.float32))
    key_grad = jnp.einsum('nhqk,nqhe->nkhe', score_grad, queries.astype(jnp.float32))
    qkv_grad = jnp.stack([query_grad, key_grad, value_grad], axis=2).astype(jnp.bfloat16)
    qkv_grad = qkv_grad.reshape(batch * length, 3 * inner)
    input_grad = jnp.dot(qkv_grad, qkv_weight.T, preferred_element_type=jnp.float32)
    norm_terms = jnp.stack([lax.optimization_barrier(jnp.sum(input_grad * normed_in, axis=0)), lax.optimization_barrier(jnp.sum(input_grad, axis=0)), merge_scale, merge_shift])
    row_grad = (hidden_grad + norm_back(input_grad, normed_in, inverse_in, ln_gain)).astype(jnp.bfloat16)
    return (row_grad, norm_terms)

def reference(patches, unit_counts, segment_ids, merged_position, ln_gain, ln_bias, qkv_weight, out_weight, merge_gain, merge_bias, merged_grad):
    source = patches.reshape(N_DP, N_CTX, SRC_UNITS, UNIT, D)
    block_ends = jnp.cumsum(unit_counts, axis=1).astype(jnp.int32)
    block_starts = (block_ends - unit_counts).astype(jnp.int32)
    wanted_block = (jnp.arange(UNITS_DEV, dtype=jnp.int32)[None, :] * N_DP + jnp.arange(N_DP, dtype=jnp.int32)[:, None]).astype(jnp.int32)
    sender_rank = lax.optimization_barrier(jnp.sum((block_ends[None, :, None, :] <= wanted_block[:, None, :, None]).astype(jnp.int32), axis=-1)).astype(jnp.int32)
    column_index = jnp.arange(N_CTX, dtype=jnp.int32)[None, :, None]
    sender_block = (wanted_block[:, None, :] - block_starts[column_index, sender_rank]).astype(jnp.int32)
    balanced = source[sender_rank, column_index, sender_block]
    labels = segment_ids.reshape(N_DP, N_CTX, ROWS)
    places = merged_position.reshape(N_DP, N_CTX * GROUPS)
    sequence_grad = merged_grad.reshape(N_DP, N_CTX, SEQ_DEV, MERGED).transpose(0, 2, 1, 3).reshape(N_DP, SEQ_DEV * N_CTX, MERGED)

    def one_rank(items):
        rows, row_labels, spots, seq_grads = items
        result, saved = block_forward(rows.reshape(N_CTX, ROWS, D), row_labels, ln_gain, ln_bias, qkv_weight, out_weight, merge_gain, merge_bias)
        tokens = result.reshape(N_CTX * GROUPS, MERGED)
        sequence = jnp.zeros((N_CTX * SEQ_DEV, MERGED), jnp.bfloat16).at[spots].set(tokens)
        upstream = seq_grads[spots].astype(jnp.float32).reshape(N_CTX * ROWS, D)
        row_grad, norm_terms = block_backward(upstream, saved, ln_gain, qkv_weight, out_weight, merge_gain)
        return (sequence, row_grad.reshape(N_CTX, UNITS_DEV, UNIT, D), norm_terms)
    sequences, row_grads, norm_terms = lax.map(one_rank, (balanced, labels, places, sequence_grad))
    merged = sequences.reshape(N_DP, SEQ_DEV, N_CTX, MERGED).transpose(0, 2, 1, 3).reshape(N_DP * N_CTX * SEQ_DEV, MERGED)
    patch_grad = jnp.zeros((N_DP, N_CTX, SRC_UNITS, UNIT, D), jnp.bfloat16).at[sender_rank, column_index, sender_block].set(row_grads)
    return (merged, patch_grad.reshape(N_DP * N_CTX * SRC_ROWS, D), lax.optimization_barrier(jnp.sum(norm_terms, axis=0)))
```

```python
import functools

import jax
import jax.numpy as jnp
from jax import lax
from jax.experimental import pallas as pl
from jax.experimental.pallas import tpu as pltpu
from jax.sharding import PartitionSpec as P

HEAD = 80
UNIT = 32
MERGE = 4
EPS = 1e-06
NEG = -1e30
LANES = 128
WIN = 256
F32 = jnp.float32
BF16 = jnp.bfloat16


def paired(size):
    return size <= 8 and size & (size - 1) == 0


def peer_of(index, slot, size):
    return index ^ slot if paired(size) else slot


def place(slot, size):
    return (slot, 0) if paired(size) else (0, slot)


def in_hbm(array):
    return pltpu.with_memory_space_constraint(array, pltpu.HBM)


def pieces(size, shape, dtype):
    if paired(size):
        return [jax.ShapeDtypeStruct((1, *shape), dtype)] * size
    return [jax.ShapeDtypeStruct((size, *shape), dtype)]


def exchange(arrays, axis, size):
    if paired(size):
        return [arrays[0]] + [
            lax.ppermute(arrays[slot], axis, [(i, i ^ slot) for i in range(size)])
            for slot in range(1, size)
        ]
    return [lax.all_to_all(arrays[0], axis, split_axis=0, concat_axis=0, tiled=True)]


def total(terms, sizes):
    dp, ctx = sizes
    if not (paired(dp) and paired(ctx)):
        return lax.psum(terms, ("dp", "ctx"))
    rounds = [("ctx", ctx, (1,)), ("ctx", ctx, range(2, ctx, 2)), ("dp", dp, range(1, dp))]
    for axis, size, slots in rounds:
        others = [
            lax.ppermute(terms, axis, [(i, i ^ slot) for i in range(size)]) for slot in slots
        ]
        for other in others:
            terms = terms + other
    return terms


def starts(counts, ranks):
    out = [jnp.int32(0)]
    for rank in range(ranks - 1):
        out.append(out[-1] + counts[rank])
    return out


def chosen(values, index):
    out = values[0]
    for i in range(1, len(values)):
        out = jnp.where(index == i, values[i], out)
    return out


def pack_blocks(sizes, capacity, where, counts, source, *rest):
    ranks = sizes[0]
    outs, sems = rest[:-1], rest[-1]
    me = where[0]
    first = chosen(starts(counts, ranks), me)
    copies = []
    for slot in range(ranks):
        array, entry = place(slot, ranks)
        lead = lax.rem(peer_of(me, slot, ranks) + 8 * ranks - first, ranks)
        for k in range(capacity):
            block = jnp.minimum(lead + k * ranks, source.shape[0] - 1)
            copies.append(
                pltpu.make_async_copy(
                    source.at[block], outs[array].at[entry, k], sems.at[slot * capacity + k]
                )
            )
            copies[-1].start()
    for copy in copies:
        copy.wait()


def moments(values):
    average = jnp.mean(values, axis=-1, keepdims=True)
    centred = values - average
    inverse = lax.rsqrt(jnp.mean(centred * centred, axis=-1, keepdims=True) + EPS)
    return centred * inverse, inverse


def norm_back(scaled, normed, inverse):
    centre = jnp.mean(scaled, axis=-1, keepdims=True)
    slope = jnp.mean(scaled * normed, axis=-1, keepdims=True)
    return inverse * (scaled - centre - normed * slope)


def dot(a, b, ca=1, cb=0):
    return lax.dot_general(a, b, (((ca,), (cb,)), ((), ())), preferred_element_type=F32)


def iota(shape, dim):
    return lax.broadcasted_iota(jnp.int32, shape, dim)


def block_kernel(sizes, capacity, *refs):
    ranks, owners = sizes
    n_in = ranks if paired(ranks) else 1
    where, counts, labels, positions, params, wq_far, wo_far = refs[:7]
    refs = refs[7:]
    arrived, refs = refs[:n_in], refs[n_in:]
    grads, refs = refs[0], refs[1:]
    back, refs = refs[:n_in], refs[n_in:]
    windows, terms, xs, qs, ks, vs, ats, ps, dqs, dks, dvs, gs, ws, rows_out, wq, wo, sems = refs
    ln_gain, ln_bias, merge_gain, merge_bias = (params[i : i + 1, :] for i in range(4))
    rows, width = xs.shape
    units = rows // UNIT
    inner = wo.shape[0]
    heads = inner // HEAD
    scale = HEAD ** (-0.5)
    tokens = rows // MERGE
    thirds = [slice(part * inner, (part + 1) * inner) for part in range(3)]
    loads = [
        pltpu.make_async_copy(wq_far.at[third], wq.at[third], sems.at[part])
        for part, third in enumerate(thirds)
    ]
    loads.append(pltpu.make_async_copy(wo_far, wo, sems.at[3]))
    for load in loads:
        load.start()
    pair = grads.shape[1]
    slots = owners * pair
    me, column = where[0], where[1]
    begin = starts(counts, ranks)

    for unit in range(units):
        wanted = unit * ranks + me
        sender = jnp.int32(0)
        for rank in range(1, ranks):
            sender = jnp.where(begin[rank] <= wanted, rank, sender)
        kth = (wanted - chosen(begin, sender)) // ranks
        span = slice(unit * UNIT, (unit + 1) * UNIT)
        if n_in == 1:
            xs[span, :] = arrived[0][sender, kth].astype(F32)
        else:
            slot = sender ^ me
            value = arrived[0][0, kth]
            for i in range(1, n_in):
                value = jnp.where(slot == i, arrived[i][0, kth], value)
            xs[span, :] = value.astype(F32)

    label = jnp.broadcast_to(labels[...].astype(F32), (rows, rows))
    joined = (label == label.T) & (
        iota((rows, rows), 0) // UNIT == iota((rows, rows), 1) // UNIT
    )
    own = iota((rows, tokens), 0) // MERGE == iota((rows, tokens), 1)
    place_of = positions[...] - column * slots
    spot = jnp.sum(jnp.where(own, place_of.astype(F32), 0.0), axis=1, keepdims=True)
    spot_row = jnp.broadcast_to(spot, (rows, LANES)).T[:1, :]
    spot = spot.astype(jnp.int32)
    spot_row = spot_row.astype(jnp.int32)

    def slot_place(index):
        local = index % slots
        return (local % pair) * owners + local // pair

    lane = iota((rows, MERGE * slots), 1)
    take = (
        (iota((rows, MERGE * slots), 0) % MERGE == lane // slots) & (slot_place(lane) == spot)
    ).astype(BF16)
    lead = iota((MERGE * slots, rows), 0)
    put = (
        (iota((MERGE * slots, rows), 1) % MERGE == lead // slots) & (slot_place(lead) == spot_row)
    ).astype(BF16)

    normed_in, inverse_in = moments(xs[...])
    shifted = (normed_in * ln_gain + ln_bias).astype(BF16)
    padded = qs.shape[1]
    zero = jnp.zeros((rows, padded - inner), BF16)
    for ref, part in ((qs, 0), (ks, 1), (vs, 2)):
        loads[part].wait()
        ref[:, :inner] = dot(shifted, wq[thirds[part], :], 1, 1).astype(BF16)
    qs[:, inner:] = zero
    ks[:, inner:] = zero
    vs[:, inner:] = zero
    ats[...] = jnp.zeros_like(ats)
    dqs[...] = jnp.zeros_like(dqs)
    dks[...] = jnp.zeros_like(dks)
    dvs[...] = jnp.zeros_like(dvs)

    win_lane = iota((rows, WIN), 1)

    def window(head):
        at = head * HEAD
        low = at // LANES * LANES
        mask = (win_lane >= at - low) & (win_lane < at - low + HEAD)
        return slice(low, low + WIN), mask

    none = jnp.zeros((), BF16)
    for head in range(heads):
        span, mask = window(head)
        scores = dot(jnp.where(mask, qs[:, span], none), ks[:, span], 1, 1) * scale
        scores = jnp.where(joined, scores, NEG)
        raised = jnp.exp(scores - jnp.max(scores, axis=-1, keepdims=True))
        prob = raised / jnp.sum(raised, axis=-1, keepdims=True)
        ps[head] = prob
        ats[:, span] += dot(prob.astype(BF16), jnp.where(mask, vs[:, span], none))
    loads[3].wait()
    hidden = xs[...] + dot(ats[:, :inner].astype(BF16), wo[...])
    normed_out, inverse_out = moments(hidden)
    result = (normed_out * merge_gain + merge_bias).astype(BF16)
    ws[...] = dot(put, result)
    for owner in range(owners):
        for part in range(MERGE):
            start = part * slots + owner * pair
            windows[owner, :, part * width : (part + 1) * width] = ws[
                start : start + pair, :
            ].astype(BF16)

    for owner in range(owners):
        for part in range(MERGE):
            start = part * slots + owner * pair
            ws[start : start + pair, :] = grads[
                owner, :, part * width : (part + 1) * width
            ].astype(F32)
    upstream = dot(take, ws[...].astype(BF16))
    terms[2:3, :] = jnp.sum(upstream * normed_out, axis=0, keepdims=True)
    terms[3:4, :] = jnp.sum(upstream, axis=0, keepdims=True)
    hidden_grad = norm_back(upstream * merge_gain, normed_out, inverse_out)
    gs[:, :inner] = dot(hidden_grad.astype(BF16), wo[...], 1, 1).astype(BF16)
    gs[:, inner:] = zero
    for head in range(heads):
        span, mask = window(head)
        prob = ps[head]
        grad = jnp.where(mask, gs[:, span], none)
        prob_grad = dot(grad, vs[:, span], 1, 1)
        dvs[:, span] += dot(prob.astype(BF16), grad, 0, 0)
        centred = prob_grad - jnp.sum(prob * prob_grad, axis=-1, keepdims=True)
        score_grad = (prob * centred * scale).astype(BF16)
        dqs[:, span] += dot(score_grad, jnp.where(mask, ks[:, span], none))
        dks[:, span] += dot(score_grad, jnp.where(mask, qs[:, span], none), 0, 0)
    input_grad = sum(
        dot(ref[:, :inner].astype(BF16), wq[thirds[part], :])
        for ref, part in ((dqs, 0), (dks, 1), (dvs, 2))
    )
    terms[0:1, :] = jnp.sum(input_grad * normed_in, axis=0, keepdims=True)
    terms[1:2, :] = jnp.sum(input_grad, axis=0, keepdims=True)
    row_grad = hidden_grad + norm_back(input_grad * ln_gain, normed_in, inverse_in)
    rows_out[...] = row_grad.astype(BF16).reshape(units, UNIT, width)

    for slot in range(ranks):
        array, entry = place(slot, ranks)
        peer = peer_of(me, slot, ranks)
        base_of = chosen(begin, peer)
        low = lax.rem(me + 8 * ranks - base_of, ranks)
        for k in range(capacity):
            unit = jnp.minimum((base_of + low + k * ranks) // ranks, units - 1)
            back[array][entry, k] = rows_out[unit]


def unpack_kernel(sizes, capacity, *refs):
    ranks = sizes[0]
    where, counts = refs[:2]
    came, patch_grad = refs[2:-1], refs[-1]
    me = where[0]
    first = chosen(starts(counts, ranks), me)
    live = chosen([counts[rank] for rank in range(ranks)], me)
    for slot in range(ranks):
        array, entry = place(slot, ranks)
        low = lax.rem(peer_of(me, slot, ranks) + 8 * ranks - first, ranks)
        for k in range(capacity):
            block = low + k * ranks

            @pl.when(block < live)
            def _(array=array, entry=entry, k=k, block=block):
                patch_grad[block] = came[array][entry, k]

            @pl.when((block >= live) & (block < patch_grad.shape[0]))
            def _(block=block):
                patch_grad[block] = jnp.zeros(patch_grad.shape[1:], BF16)


def per_device(
    sizes,
    patches,
    unit_counts,
    segment_ids,
    merged_position,
    ln_gain,
    ln_bias,
    qkv_weight,
    out_weight,
    merge_gain,
    merge_bias,
    merged_grad,
):
    ranks, owners = sizes
    width = patches.shape[1]
    source_units = patches.shape[0] // UNIT
    rows = segment_ids.shape[0]
    capacity = -(-source_units // ranks)
    owner_slots, token_width = merged_grad.shape
    pair = owner_slots // owners
    inner = out_weight.shape[0]
    heads = inner // HEAD
    padded = -(-inner // LANES) * LANES
    where = jnp.stack([lax.axis_index("dp"), lax.axis_index("ctx")]).astype(jnp.int32)
    counts = unit_counts.reshape(-1)
    smem = pl.BlockSpec(memory_space=pltpu.SMEM)
    vmem = pl.BlockSpec(memory_space=pltpu.VMEM)
    anywhere = pl.BlockSpec(memory_space=pl.ANY)

    block_shapes = pieces(ranks, (capacity, UNIT, width), BF16)
    window_shape = jax.ShapeDtypeStruct((owners, pair, token_width), BF16)
    n_in = len(block_shapes)
    swap = functools.partial(
        lax.all_to_all, axis_name="ctx", split_axis=0, concat_axis=0, tiled=True
    )

    outgoing = pl.pallas_call(
        functools.partial(pack_blocks, sizes, capacity),
        out_shape=block_shapes,
        in_specs=[smem, smem, anywhere],
        out_specs=[vmem] * n_in,
        scratch_shapes=[pltpu.SemaphoreType.DMA((ranks * capacity,))],
        compiler_params=pltpu.CompilerParams(vmem_limit_bytes=4 * 2**20),
        name="pack_blocks",
    )(
        in_hbm(where),
        in_hbm(counts),
        in_hbm(patches.reshape(source_units, UNIT, width)),
    )
    arrived = exchange(outgoing, "dp", ranks)

    grad_blocks = merged_grad.reshape(owners, pair, token_width)
    grads = swap(grad_blocks)

    results = pl.pallas_call(
        functools.partial(block_kernel, sizes, capacity),
        out_shape=[
            *block_shapes,
            window_shape,
            jax.ShapeDtypeStruct((4, width), F32),
        ],
        in_specs=[smem, smem] + [vmem] * 3 + [anywhere] * 2 + [vmem] * (n_in + 1),
        out_specs=[vmem] * (n_in + 2),
        scratch_shapes=[
            pltpu.VMEM((rows, width), F32),
            pltpu.VMEM((rows, padded), BF16),
            pltpu.VMEM((rows, padded), BF16),
            pltpu.VMEM((rows, padded), BF16),
            pltpu.VMEM((rows, padded), F32),
            pltpu.VMEM((heads, rows, rows), F32),
            pltpu.VMEM((rows, padded), F32),
            pltpu.VMEM((rows, padded), F32),
            pltpu.VMEM((rows, padded), F32),
            pltpu.VMEM((rows, padded), BF16),
            pltpu.VMEM((MERGE * owners * pair, width), F32),
            pltpu.VMEM((rows // UNIT, UNIT, width), BF16),
            pltpu.VMEM((3 * inner, width), BF16),
            pltpu.VMEM((inner, width), BF16),
            pltpu.SemaphoreType.DMA((4,)),
        ],
        compiler_params=pltpu.CompilerParams(vmem_limit_bytes=40 * 2**20),
        cost_estimate=pl.CostEstimate(
            flops=3 * 10**9, bytes_accessed=12 * 10**6, transcendentals=200_000
        ),
        name="block",
    )(
        in_hbm(where),
        in_hbm(counts),
        in_hbm(segment_ids.reshape(1, rows)),
        in_hbm(merged_position.reshape(1, rows // MERGE)),
        in_hbm(jnp.stack([ln_gain, ln_bias, merge_gain, merge_bias])),
        in_hbm(qkv_weight.T),
        in_hbm(out_weight),
        in_hbm(arrived[0]),
        *arrived[1:],
        grads,
    )
    came_back = exchange(results[:n_in], "dp", ranks)
    merged = swap(results[n_in])
    norm_grads = total(results[-1], sizes)
    patch_grad = pl.pallas_call(
        functools.partial(unpack_kernel, sizes, capacity),
        out_shape=jax.ShapeDtypeStruct((source_units, UNIT, width), BF16),
        in_specs=[smem, smem] + [vmem] * n_in,
        out_specs=vmem,
        compiler_params=pltpu.CompilerParams(vmem_limit_bytes=8 * 2**20),
        name="unpack",
    )(in_hbm(where), in_hbm(counts), in_hbm(came_back[0]), *came_back[1:])
    return (
        merged.reshape(owner_slots, token_width),
        patch_grad.reshape(source_units * UNIT, width),
        norm_grads,
    )


def solution(mesh):
    return jax.shard_map(
        functools.partial(per_device, (mesh.shape["dp"], mesh.shape["ctx"])),
        mesh=mesh,
        in_specs=(
            P(("dp", "ctx"), None),
            P("ctx", None),
            P(("dp", "ctx")),
            P(("dp", "ctx")),
            P(),
            P(),
            P(),
            P(),
            P(),
            P(),
            P(("dp", "ctx"), None),
        ),
        out_specs=(P(("dp", "ctx"), None), P(("dp", "ctx"), None), P()),
        check_vma=False,
    )
```

```python
import functools

import jax
import jax.numpy as jnp
from jax import lax
from jax.experimental import pallas as pl
from jax.experimental.pallas import tpu as pltpu
from jax.sharding import PartitionSpec as P

HEAD = 80
UNIT = 32
MERGE = 4
EPS = 1e-06
NEG = -1e30
LANES = 128
WIN = 256
F32 = jnp.float32
BF16 = jnp.bfloat16
FRONT_FLOPS = 12 * 10**9
UNPACK_FLOPS = 10**10


def paired(size):
    return size <= 8 and size & (size - 1) == 0


def peer_of(index, slot, size):
    return index ^ slot if paired(size) else slot


def place(slot, size):
    return (slot, 0) if paired(size) else (0, slot)


def in_hbm(array):
    return pltpu.with_memory_space_constraint(array, pltpu.HBM)


def pieces(size, shape, dtype):
    if paired(size):
        return [pltpu.HBM((1, *shape), dtype)] + [
            jax.ShapeDtypeStruct((1, *shape), dtype)
        ] * (size - 1)
    return [jax.ShapeDtypeStruct((size, *shape), dtype)]


def exchange(arrays, axis, size):
    if paired(size):
        return [arrays[0]] + [
            lax.ppermute(arrays[slot], axis, [(i, i ^ slot) for i in range(size)])
            for slot in range(1, size)
        ]
    return [lax.all_to_all(arrays[0], axis, split_axis=0, concat_axis=0, tiled=True)]


def spread(terms, axis, size, slots):
    others = [
        lax.ppermute(terms, axis, [(i, i ^ slot) for i in range(size)]) for slot in slots
    ]
    for other in others:
        terms = terms + other
    return terms


def starts(counts, ranks):
    out = [jnp.int32(0)]
    for rank in range(ranks - 1):
        out.append(out[-1] + counts[rank])
    return out


def chosen(values, index):
    out = values[0]
    for i in range(1, len(values)):
        out = jnp.where(index == i, values[i], out)
    return out


def pack_blocks(sizes, capacity, where, counts, source, *rest):
    ranks = sizes[0]
    outs, sems = rest[:-1], rest[-1]
    me = where[0]
    first = chosen(starts(counts, ranks), me)
    copies = []
    for slot in range(ranks):
        array, entry = place(slot, ranks)
        lead = lax.rem(peer_of(me, slot, ranks) + 8 * ranks - first, ranks)
        for k in range(capacity):
            block = jnp.minimum(lead + k * ranks, source.shape[0] - 1)
            copies.append(
                pltpu.make_async_copy(
                    source.at[block], outs[array].at[entry, k], sems.at[slot * capacity + k]
                )
            )
            copies[-1].start()
    for copy in copies:
        copy.wait()


def moments(values):
    average = jnp.mean(values, axis=-1, keepdims=True)
    centred = values - average
    inverse = lax.rsqrt(jnp.mean(centred * centred, axis=-1, keepdims=True) + EPS)
    return centred * inverse, inverse


def norm_back(scaled, normed, inverse):
    centre = jnp.mean(scaled, axis=-1, keepdims=True)
    slope = jnp.mean(scaled * normed, axis=-1, keepdims=True)
    return inverse * (scaled - centre - normed * slope)


def dot(a, b, ca=1, cb=0):
    return lax.dot_general(a, b, (((ca,), (cb,)), ((), ())), preferred_element_type=F32)


def iota(shape, dim):
    return lax.broadcasted_iota(jnp.int32, shape, dim)


def front_kernel(sizes, capacity, *refs):
    ranks = sizes[0]
    n_in = ranks if paired(ranks) else 1
    where, counts, ln_gain, ln_bias, wq_far = refs[:5]
    arrived, refs = refs[5 : 5 + n_in], refs[5 + n_in :]
    xs, normed_ref, inverse_ref, qs, ks, vs, wq, sems = refs
    rows, width = xs.shape
    units = rows // UNIT
    inner = wq.shape[0] // 3
    thirds = [slice(part * inner, (part + 1) * inner) for part in range(3)]
    loads = [
        pltpu.make_async_copy(wq_far.at[third], wq.at[third], sems.at[part])
        for part, third in enumerate(thirds)
    ]
    for load in loads:
        load.start()
    me = where[0]
    begin = starts(counts, ranks)
    for unit in range(units):
        wanted = unit * ranks + me
        sender = jnp.int32(0)
        for rank in range(1, ranks):
            sender = jnp.where(begin[rank] <= wanted, rank, sender)
        kth = (wanted - chosen(begin, sender)) // ranks
        span = slice(unit * UNIT, (unit + 1) * UNIT)
        if n_in == 1:
            xs[span, :] = arrived[0][sender, kth]
        else:
            slot = sender ^ me
            value = arrived[0][0, kth]
            for i in range(1, n_in):
                value = jnp.where(slot == i, arrived[i][0, kth], value)
            xs[span, :] = value
    normed, inverse = moments(xs[...].astype(F32))
    normed_ref[...] = normed
    inverse_ref[...] = jnp.broadcast_to(inverse, inverse_ref.shape)
    gain, bias = ln_gain[...].reshape(1, width), ln_bias[...].reshape(1, width)
    shifted = (normed * gain + bias).astype(BF16)
    for ref, part in ((qs, 0), (ks, 1), (vs, 2)):
        ref[:, inner:] = jnp.zeros((rows, ref.shape[1] - inner), BF16)
        loads[part].wait()
        ref[:, :inner] = dot(shifted, wq[thirds[part], :], 1, 1).astype(BF16)


def block_kernel(sizes, capacity, *refs):
    ranks, owners = sizes
    n_in = ranks if paired(ranks) else 1
    where, counts, labels, positions, *params, wq_far, wo_far = refs[:9]
    xs, normed_ref, inverse_ref, qs, ks, vs, grads = refs[9:16]
    refs = refs[16:]
    back, refs = refs[:n_in], refs[n_in:]
    windows, terms_out, ats, ps, dqs, dks, dvs, gs, ws, rows_out, terms, wq, wo, sems = refs
    rows, width = xs.shape
    ln_gain, merge_gain, merge_bias = (ref[...].reshape(1, width) for ref in params)
    units = rows // UNIT
    inner = wo.shape[0]
    heads = inner // HEAD
    scale = HEAD ** (-0.5)
    tokens = rows // MERGE
    loads = [
        pltpu.make_async_copy(wo_far, wo, sems.at[0]),
        pltpu.make_async_copy(wq_far, wq, sems.at[1]),
    ]
    for load in loads:
        load.start()
    pair = grads.shape[1]
    slots = owners * pair
    me, column = where[0], where[1]
    begin = starts(counts, ranks)
    normed_in, inverse_in = normed_ref[...], inverse_ref[:, :1]

    label = jnp.broadcast_to(labels[...].astype(F32), (rows, rows))
    joined = (label == label.T) & (
        iota((rows, rows), 0) // UNIT == iota((rows, rows), 1) // UNIT
    )
    own = iota((rows, tokens), 0) // MERGE == iota((rows, tokens), 1)
    place_of = positions[...] - column * slots
    spot = jnp.sum(jnp.where(own, place_of.astype(F32), 0.0), axis=1, keepdims=True)
    spot_row = jnp.broadcast_to(spot, (rows, LANES)).T[:1, :]
    spot = spot.astype(jnp.int32)
    spot_row = spot_row.astype(jnp.int32)

    def slot_place(index):
        local = index % slots
        return (local % pair) * owners + local // pair

    lane = iota((rows, MERGE * slots), 1)
    take = (
        (iota((rows, MERGE * slots), 0) % MERGE == lane // slots) & (slot_place(lane) == spot)
    ).astype(BF16)
    lead = iota((MERGE * slots, rows), 0)
    put = (
        (iota((MERGE * slots, rows), 1) % MERGE == lead // slots) & (slot_place(lead) == spot_row)
    ).astype(BF16)

    zero = jnp.zeros((rows, gs.shape[1] - inner), BF16)
    ats[...] = jnp.zeros_like(ats)
    dqs[...] = jnp.zeros_like(dqs)
    dks[...] = jnp.zeros_like(dks)
    dvs[...] = jnp.zeros_like(dvs)

    win_lane = iota((rows, WIN), 1)

    def window(head):
        at = head * HEAD
        low = at // LANES * LANES
        mask = (win_lane >= at - low) & (win_lane < at - low + HEAD)
        return slice(low, low + WIN), mask

    none = jnp.zeros((), BF16)
    for head in range(heads):
        span, mask = window(head)
        scores = dot(jnp.where(mask, qs[:, span], none), ks[:, span], 1, 1) * scale
        scores = jnp.where(joined, scores, NEG)
        raised = jnp.exp(scores - jnp.max(scores, axis=-1, keepdims=True))
        prob = raised / jnp.sum(raised, axis=-1, keepdims=True)
        ps[head] = prob
        ats[:, span] += dot(prob.astype(BF16), jnp.where(mask, vs[:, span], none))
    loads[0].wait()
    hidden = xs[...].astype(F32) + dot(ats[:, :inner].astype(BF16), wo[...])
    normed_out, inverse_out = moments(hidden)
    result = (normed_out * merge_gain + merge_bias).astype(BF16)
    ws[...] = dot(put, result)
    for owner in range(owners):
        for part in range(MERGE):
            start = part * slots + owner * pair
            windows[owner, :, part * width : (part + 1) * width] = ws[
                start : start + pair, :
            ].astype(BF16)

    for owner in range(owners):
        for part in range(MERGE):
            start = part * slots + owner * pair
            ws[start : start + pair, :] = grads[
                owner, :, part * width : (part + 1) * width
            ].astype(F32)
    upstream = dot(take, ws[...].astype(BF16))
    terms[2:3, :] = jnp.sum(upstream * normed_out, axis=0, keepdims=True)
    terms[3:4, :] = jnp.sum(upstream, axis=0, keepdims=True)
    hidden_grad = norm_back(upstream * merge_gain, normed_out, inverse_out)
    gs[:, :inner] = dot(hidden_grad.astype(BF16), wo[...], 1, 1).astype(BF16)
    gs[:, inner:] = zero
    for head in range(heads):
        span, mask = window(head)
        prob = ps[head]
        grad = jnp.where(mask, gs[:, span], none)
        prob_grad = dot(grad, vs[:, span], 1, 1)
        dvs[:, span] += dot(prob.astype(BF16), grad, 0, 0)
        centred = prob_grad - jnp.sum(prob * prob_grad, axis=-1, keepdims=True)
        score_grad = (prob * centred * scale).astype(BF16)
        dqs[:, span] += dot(score_grad, jnp.where(mask, ks[:, span], none))
        dks[:, span] += dot(score_grad, jnp.where(mask, qs[:, span], none), 0, 0)
    loads[1].wait()
    input_grad = sum(
        dot(ref[:, :inner].astype(BF16), wq[part * inner : (part + 1) * inner, :])
        for ref, part in ((dqs, 0), (dks, 1), (dvs, 2))
    )
    terms[0:1, :] = jnp.sum(input_grad * normed_in, axis=0, keepdims=True)
    terms[1:2, :] = jnp.sum(input_grad, axis=0, keepdims=True)
    row_grad = hidden_grad + norm_back(input_grad * ln_gain, normed_in, inverse_in)
    rows_out[...] = row_grad.astype(BF16).reshape(units, UNIT, width)

    terms_out[...] = terms[...]
    spare = windows.shape[2] - MERGE * width
    if spare:
        high = terms[...].astype(BF16)
        low = (terms[...] - high.astype(F32)).astype(BF16)
        for owner in range(owners):
            windows[owner, :, MERGE * width :] = jnp.concatenate([high, low], axis=0)

    for slot in range(ranks):
        array, entry = place(slot, ranks)
        peer = peer_of(me, slot, ranks)
        base_of = chosen(begin, peer)
        low = lax.rem(me + 8 * ranks - base_of, ranks)
        for k in range(capacity):
            unit = jnp.minimum((base_of + low + k * ranks) // ranks, units - 1)
            back[array][entry, k] = rows_out[unit]


def unpack_kernel(sizes, capacity, *refs):
    ranks = sizes[0]
    where, counts = refs[:2]
    came, patch_grad = refs[2:-1], refs[-1]
    me = where[0]
    first = chosen(starts(counts, ranks), me)
    live = chosen([counts[rank] for rank in range(ranks)], me)
    for slot in range(ranks):
        array, entry = place(slot, ranks)
        low = lax.rem(peer_of(me, slot, ranks) + 8 * ranks - first, ranks)
        for k in range(capacity):
            block = low + k * ranks

            @pl.when(block < live)
            def _(array=array, entry=entry, k=k, block=block):
                patch_grad[block] = came[array][entry, k]

            @pl.when((block >= live) & (block < patch_grad.shape[0]))
            def _(block=block):
                patch_grad[block] = jnp.zeros(patch_grad.shape[1:], BF16)


def per_device(
    sizes,
    patches,
    unit_counts,
    segment_ids,
    merged_position,
    ln_gain,
    ln_bias,
    qkv_weight,
    out_weight,
    merge_gain,
    merge_bias,
    merged_grad,
):
    ranks, owners = sizes
    width = patches.shape[1]
    source_units = patches.shape[0] // UNIT
    rows = segment_ids.shape[0]
    capacity = -(-source_units // ranks)
    owner_slots, token_width = merged_grad.shape
    pair = owner_slots // owners
    inner = out_weight.shape[0]
    heads = inner // HEAD
    padded = -(-inner // LANES) * LANES
    where = jnp.stack([lax.axis_index("dp"), lax.axis_index("ctx")]).astype(jnp.int32)
    counts = unit_counts.reshape(-1)
    smem = pl.BlockSpec(memory_space=pltpu.SMEM)
    vmem = pl.BlockSpec(memory_space=pltpu.VMEM)
    anywhere = pl.BlockSpec(memory_space=pl.ANY)

    block_shapes = pieces(ranks, (capacity, UNIT, width), BF16)
    beside = paired(ranks) and paired(owners) and pair == 8
    window_shape = jax.ShapeDtypeStruct(
        (owners, pair, token_width + (width if beside else 0)), BF16
    )
    n_in = len(block_shapes)
    swap = functools.partial(
        lax.all_to_all, axis_name="ctx", split_axis=0, concat_axis=0, tiled=True
    )

    outgoing = pl.pallas_call(
        functools.partial(pack_blocks, sizes, capacity),
        out_shape=block_shapes,
        in_specs=[smem, smem, anywhere],
        out_specs=[vmem] * n_in,
        scratch_shapes=[pltpu.SemaphoreType.DMA((ranks * capacity,))],
        compiler_params=pltpu.CompilerParams(vmem_limit_bytes=4 * 2**20),
        name="pack_blocks",
    )(
        in_hbm(where),
        in_hbm(counts),
        in_hbm(patches.reshape(source_units, UNIT, width)),
    )
    arrived = exchange(outgoing, "dp", ranks)

    grad_blocks = merged_grad.reshape(owners, pair, token_width)
    grads = swap(grad_blocks)

    wide = jax.ShapeDtypeStruct((rows, padded), BF16)
    state = pl.pallas_call(
        functools.partial(front_kernel, sizes, capacity),
        out_shape=[
            jax.ShapeDtypeStruct((rows, width), BF16),
            jax.ShapeDtypeStruct((rows, width), F32),
            jax.ShapeDtypeStruct((rows, LANES), F32),
            wide,
            wide,
            wide,
        ],
        in_specs=[smem] * 2 + [vmem] * 2 + [anywhere] + [vmem] * n_in,
        out_specs=[vmem] * 6,
        scratch_shapes=[
            pltpu.VMEM((3 * inner, width), BF16),
            pltpu.SemaphoreType.DMA((3,)),
        ],
        compiler_params=pltpu.CompilerParams(vmem_limit_bytes=24 * 2**20),
        cost_estimate=pl.CostEstimate(
            flops=FRONT_FLOPS, bytes_accessed=8 * 10**6, transcendentals=0
        ),
        name="front",
    )(
        *map(in_hbm, (where, counts, ln_gain, ln_bias, qkv_weight.T, arrived[0])),
        *arrived[1:],
    )

    results = pl.pallas_call(
        functools.partial(block_kernel, sizes, capacity),
        out_shape=[
            *block_shapes,
            window_shape,
            jax.ShapeDtypeStruct((4, width), F32),
        ],
        in_specs=[smem] * 2 + [vmem] * 5 + [anywhere] * 2 + [vmem] * 7,
        out_specs=[vmem] * (n_in + 2),
        scratch_shapes=[
            pltpu.VMEM((rows, padded), F32),
            pltpu.VMEM((heads, rows, rows), F32),
            pltpu.VMEM((rows, padded), F32),
            pltpu.VMEM((rows, padded), F32),
            pltpu.VMEM((rows, padded), F32),
            pltpu.VMEM((rows, padded), BF16),
            pltpu.VMEM((MERGE * owners * pair, width), F32),
            pltpu.VMEM((rows // UNIT, UNIT, width), BF16),
            pltpu.VMEM((4, width), F32),
            pltpu.VMEM((3 * inner, width), BF16),
            pltpu.VMEM((inner, width), BF16),
            pltpu.SemaphoreType.DMA((2,)),
        ],
        compiler_params=pltpu.CompilerParams(vmem_limit_bytes=40 * 2**20),
        cost_estimate=pl.CostEstimate(
            flops=2 * 10**9, bytes_accessed=12 * 10**6, transcendentals=200_000
        ),
        name="block",
    )(
        *map(
            in_hbm,
            (
                where,
                counts,
                segment_ids.reshape(1, rows),
                merged_position.reshape(1, rows // MERGE),
                ln_gain,
                merge_gain,
                merge_bias,
                qkv_weight.T,
                out_weight,
            ),
        ),
        *state,
        grads,
    )
    came_back = exchange(results[:n_in], "dp", ranks)
    merged = swap(results[n_in])
    patch_grad = pl.pallas_call(
        functools.partial(unpack_kernel, sizes, capacity),
        out_shape=jax.ShapeDtypeStruct((source_units, UNIT, width), BF16),
        in_specs=[smem, smem] + [vmem] * n_in,
        out_specs=vmem,
        compiler_params=pltpu.CompilerParams(vmem_limit_bytes=8 * 2**20),
        cost_estimate=pl.CostEstimate(
            flops=UNPACK_FLOPS, bytes_accessed=10**6, transcendentals=0
        ),
        name="unpack",
    )(in_hbm(where), in_hbm(counts), in_hbm(came_back[0]), *came_back[1:])
    if beside:
        halves = merged[:, :, token_width:].astype(F32)
        terms = jnp.sum(halves[:, :4] + halves[:, 4:], axis=0)
        terms, patch_grad = lax.optimization_barrier((terms, patch_grad))
        norm_grads = spread(terms, "dp", ranks, range(1, ranks))
        merged = merged[:, :, :token_width]
    else:
        norm_grads = lax.psum(results[-1], ("dp", "ctx"))
    return (
        merged.reshape(owner_slots, token_width),
        patch_grad.reshape(source_units * UNIT, width),
        norm_grads,
    )


def solution(mesh):
    return jax.shard_map(
        functools.partial(per_device, (mesh.shape["dp"], mesh.shape["ctx"])),
        mesh=mesh,
        in_specs=(
            P(("dp", "ctx"), None),
            P("ctx", None),
            P(("dp", "ctx")),
            P(("dp", "ctx")),
            P(),
            P(),
            P(),
            P(),
            P(),
            P(),
            P(("dp", "ctx"), None),
        ),
        out_specs=(P(("dp", "ctx"), None), P(("dp", "ctx"), None), P()),
        check_vma=False,
    )
```

```python
import functools

import jax
import jax.numpy as jnp
from jax import lax
from jax.experimental import pallas as pl
from jax.experimental.pallas import tpu as pltpu
from jax.sharding import PartitionSpec as P

HEAD = 80
UNIT = 32
MERGE = 4
EPS = 1e-06
NEG = -1e30
LANES = 128
WIN = 256
F32 = jnp.float32
BF16 = jnp.bfloat16
FRONT_FLOPS = 12 * 10**9
HOLD_PARTS = 6
HOLD_FLOPS = 10**8
UNPACK_FLOPS = 10**10


def paired(size):
    return size <= 8 and size & (size - 1) == 0


def peer_of(index, slot, size):
    return index ^ slot if paired(size) else slot


def place(slot, size):
    return (slot, 0) if paired(size) else (0, slot)


def in_hbm(array):
    return pltpu.with_memory_space_constraint(array, pltpu.HBM)


def pieces(size, shape, dtype):
    if paired(size):
        return [pltpu.HBM((1, *shape), dtype)] + [
            jax.ShapeDtypeStruct((1, *shape), dtype)
        ] * (size - 1)
    return [jax.ShapeDtypeStruct((size, *shape), dtype)]


def exchange(arrays, axis, size):
    if paired(size):
        return [arrays[0]] + [
            lax.ppermute(arrays[slot], axis, [(i, i ^ slot) for i in range(size)])
            for slot in range(1, size)
        ]
    return [lax.all_to_all(arrays[0], axis, split_axis=0, concat_axis=0, tiled=True)]


def spread(terms, axis, size, slots):
    others = [
        lax.ppermute(terms, axis, [(i, i ^ slot) for i in range(size)]) for slot in slots
    ]
    for other in others:
        terms = terms + other
    return terms


def starts(counts, ranks):
    out = [jnp.int32(0)]
    for rank in range(ranks - 1):
        out.append(out[-1] + counts[rank])
    return out


def chosen(values, index):
    out = values[0]
    for i in range(1, len(values)):
        out = jnp.where(index == i, values[i], out)
    return out


def pack_blocks(sizes, capacity, counts, source, *rest):
    ranks = sizes[0]
    outs, sems = rest[:-1], rest[-1]
    me = lax.axis_index("dp")
    first = chosen(starts(counts, ranks), me)
    copies = []
    for slot in range(ranks):
        array, entry = place(slot, ranks)
        lead = lax.rem(peer_of(me, slot, ranks) + 8 * ranks - first, ranks)
        for k in range(capacity):
            block = jnp.minimum(lead + k * ranks, source.shape[0] - 1)
            copies.append(
                pltpu.make_async_copy(
                    source.at[block], outs[array].at[entry, k], sems.at[slot * capacity + k]
                )
            )
            copies[-1].start()
    for copy in copies:
        copy.wait()


def hold(far, near, sems):
    count = sems.shape[0]
    step = far.shape[0] // count
    spans = [slice(i * step, (i + 1) * step) for i in range(count)]
    copies = [
        pltpu.make_async_copy(far.at[span], near.at[span], sems.at[i])
        for i, span in enumerate(spans)
    ]
    for copy in copies:
        copy.start()
    for copy in copies:
        copy.wait()


def moments(values):
    average = jnp.mean(values, axis=-1, keepdims=True)
    centred = values - average
    inverse = lax.rsqrt(jnp.mean(centred * centred, axis=-1, keepdims=True) + EPS)
    return centred * inverse, inverse


def norm_back(scaled, normed, inverse):
    centre = jnp.mean(scaled, axis=-1, keepdims=True)
    slope = jnp.mean(scaled * normed, axis=-1, keepdims=True)
    return inverse * (scaled - centre - normed * slope)


def dot(a, b, ca=1, cb=0):
    return lax.dot_general(a, b, (((ca,), (cb,)), ((), ())), preferred_element_type=F32)


def iota(shape, dim):
    return lax.broadcasted_iota(jnp.int32, shape, dim)


def front_kernel(sizes, capacity, *refs):
    ranks = sizes[0]
    n_in = ranks if paired(ranks) else 1
    counts, ln_gain, ln_bias, wq = refs[:4]
    arrived, refs = refs[4 : 4 + n_in], refs[4 + n_in :]
    xs, normed_ref, inverse_ref, qs, ks, vs = refs
    rows, width = xs.shape
    units = rows // UNIT
    inner = wq.shape[0] // 3
    thirds = [slice(part * inner, (part + 1) * inner) for part in range(3)]
    me = lax.axis_index("dp")
    begin = starts(counts, ranks)
    for unit in range(units):
        wanted = unit * ranks + me
        sender = jnp.int32(0)
        for rank in range(1, ranks):
            sender = jnp.where(begin[rank] <= wanted, rank, sender)
        kth = (wanted - chosen(begin, sender)) // ranks
        span = slice(unit * UNIT, (unit + 1) * UNIT)
        if n_in == 1:
            xs[span, :] = arrived[0][sender, kth]
        else:
            slot = sender ^ me
            value = arrived[0][0, kth]
            for i in range(1, n_in):
                value = jnp.where(slot == i, arrived[i][0, kth], value)
            xs[span, :] = value
    normed, inverse = moments(xs[...].astype(F32))
    normed_ref[...] = normed
    inverse_ref[...] = jnp.broadcast_to(inverse, inverse_ref.shape)
    gain, bias = ln_gain[...].reshape(1, width), ln_bias[...].reshape(1, width)
    shifted = (normed * gain + bias).astype(BF16)
    for ref, part in ((qs, 0), (ks, 1), (vs, 2)):
        ref[:, inner:] = jnp.zeros((rows, ref.shape[1] - inner), BF16)
        ref[:, :inner] = dot(shifted, wq[thirds[part], :], 1, 1).astype(BF16)


def block_kernel(sizes, capacity, *refs):
    ranks, owners = sizes
    n_in = ranks if paired(ranks) else 1
    counts, labels, positions, *params, wq_far, wo_far = refs[:8]
    xs, normed_ref, inverse_ref, qs, ks, vs, grads = refs[8:15]
    refs = refs[15:]
    back, refs = refs[:n_in], refs[n_in:]
    windows, terms_out, ats, ps, dqs, dks, dvs, gs, ws, rows_out, terms, wq, wo, sems = refs
    rows, width = xs.shape
    ln_gain, merge_gain, merge_bias = (ref[...].reshape(1, width) for ref in params)
    units = rows // UNIT
    inner = wo.shape[0]
    heads = inner // HEAD
    scale = HEAD ** (-0.5)
    tokens = rows // MERGE
    load_out = pltpu.make_async_copy(wo_far, wo, sems.at[0])
    load_qkv = pltpu.make_async_copy(wq_far, wq, sems.at[1])
    load_out.start()
    load_qkv.start()
    pair = grads.shape[1]
    slots = owners * pair
    me, column = lax.axis_index("dp"), lax.axis_index("ctx")
    begin = starts(counts, ranks)
    normed_in, inverse_in = normed_ref[...], inverse_ref[:, :1]

    label = jnp.broadcast_to(labels[...].astype(F32), (rows, rows))
    joined = (label == label.T) & (
        iota((rows, rows), 0) // UNIT == iota((rows, rows), 1) // UNIT
    )
    own = iota((rows, tokens), 0) // MERGE == iota((rows, tokens), 1)
    place_of = positions[...] - column * slots
    spot = jnp.sum(jnp.where(own, place_of.astype(F32), 0.0), axis=1, keepdims=True)
    spot_row = jnp.broadcast_to(spot, (rows, LANES)).T[:1, :]
    spot = spot.astype(jnp.int32)
    spot_row = spot_row.astype(jnp.int32)

    def slot_place(index):
        local = index % slots
        return (local % pair) * owners + local // pair

    lane = iota((rows, MERGE * slots), 1)
    take = (
        (iota((rows, MERGE * slots), 0) % MERGE == lane // slots) & (slot_place(lane) == spot)
    ).astype(BF16)
    lead = iota((MERGE * slots, rows), 0)
    put = (
        (iota((MERGE * slots, rows), 1) % MERGE == lead // slots) & (slot_place(lead) == spot_row)
    ).astype(BF16)

    zero = jnp.zeros((rows, gs.shape[1] - inner), BF16)
    ats[...] = jnp.zeros_like(ats)
    dqs[...] = jnp.zeros_like(dqs)
    dks[...] = jnp.zeros_like(dks)
    dvs[...] = jnp.zeros_like(dvs)

    win_lane = iota((rows, WIN), 1)
    none = jnp.zeros((), BF16)

    def window(two):
        at = 2 * two * HEAD
        low = at // LANES * LANES
        first = (win_lane >= at - low) & (win_lane < at - low + HEAD)
        second = (win_lane >= at - low + HEAD) & (win_lane < at - low + 2 * HEAD)
        return slice(low, low + WIN), first, second

    def stacked(value, first, second):
        return jnp.concatenate(
            [jnp.where(first, value, none), jnp.where(second, value, none)], axis=0
        )

    def own_part(value, first, second):
        return jnp.where(first, value[:rows], jnp.where(second, value[rows:], 0.0))

    for two in range(heads // 2):
        span, first, second = window(two)
        scores = dot(qs[:, span], stacked(ks[:, span], first, second), 1, 1) * scale
        for side in range(2):
            half = slice(side * rows, (side + 1) * rows)
            score = jnp.where(joined, scores[:, half], NEG)
            raised = jnp.exp(score - jnp.max(score, axis=-1, keepdims=True))
            ps[two, :, half] = raised / jnp.sum(raised, axis=-1, keepdims=True)
        ats[:, span] += dot(ps[two].astype(BF16), stacked(vs[:, span], first, second))
    load_out.wait()
    hidden = xs[...].astype(F32) + dot(ats[:, :inner].astype(BF16), wo[...])
    normed_out, inverse_out = moments(hidden)
    result = (normed_out * merge_gain + merge_bias).astype(BF16)
    ws[...] = dot(put, result)
    for owner in range(owners):
        for part in range(MERGE):
            start = part * slots + owner * pair
            windows[owner, :, part * width : (part + 1) * width] = ws[
                start : start + pair, :
            ].astype(BF16)

    for owner in range(owners):
        for part in range(MERGE):
            start = part * slots + owner * pair
            ws[start : start + pair, :] = grads[
                owner, :, part * width : (part + 1) * width
            ].astype(F32)
    upstream = dot(take, ws[...].astype(BF16))
    terms[2:3, :] = jnp.sum(upstream * normed_out, axis=0, keepdims=True)
    terms[3:4, :] = jnp.sum(upstream, axis=0, keepdims=True)
    hidden_grad = norm_back(upstream * merge_gain, normed_out, inverse_out)
    gs[:, :inner] = dot(hidden_grad.astype(BF16), wo[...], 1, 1).astype(BF16)
    gs[:, inner:] = zero
    for two in range(heads // 2):
        span, first, second = window(two)
        prob = ps[two]
        grad = gs[:, span]
        prob_grad = dot(grad, stacked(vs[:, span], first, second), 1, 1)
        dvs[:, span] += own_part(dot(prob.astype(BF16), grad, 0, 0), first, second)
        weighted = prob * prob_grad
        centred = [
            prob_grad[:, half] - jnp.sum(weighted[:, half], axis=-1, keepdims=True)
            for half in (slice(0, rows), slice(rows, 2 * rows))
        ]
        score_grad = (prob * jnp.concatenate(centred, axis=1) * scale).astype(BF16)
        dqs[:, span] += dot(score_grad, stacked(ks[:, span], first, second))
        dks[:, span] += own_part(dot(score_grad, qs[:, span], 0, 0), first, second)
    load_qkv.wait()
    input_grad = sum(
        dot(ref[:, :inner].astype(BF16), wq[part * inner : (part + 1) * inner, :])
        for ref, part in ((dqs, 0), (dks, 1), (dvs, 2))
    )
    terms[0:1, :] = jnp.sum(input_grad * normed_in, axis=0, keepdims=True)
    terms[1:2, :] = jnp.sum(input_grad, axis=0, keepdims=True)
    row_grad = hidden_grad + norm_back(input_grad * ln_gain, normed_in, inverse_in)
    rows_out[...] = row_grad.astype(BF16).reshape(units, UNIT, width)

    terms_out[...] = terms[...]
    spare = windows.shape[2] - MERGE * width
    if spare:
        high = terms[...].astype(BF16)
        low = (terms[...] - high.astype(F32)).astype(BF16)
        for owner in range(owners):
            windows[owner, :, MERGE * width :] = jnp.concatenate([high, low], axis=0)

    for slot in range(ranks):
        array, entry = place(slot, ranks)
        peer = peer_of(me, slot, ranks)
        base_of = chosen(begin, peer)
        low = lax.rem(me + 8 * ranks - base_of, ranks)
        for k in range(capacity):
            unit = jnp.minimum((base_of + low + k * ranks) // ranks, units - 1)
            back[array][entry, k] = rows_out[unit]


def unpack_kernel(sizes, capacity, *refs):
    ranks = sizes[0]
    counts, *came, patch_grad = refs
    me = lax.axis_index("dp")
    first = chosen(starts(counts, ranks), me)
    live = chosen([counts[rank] for rank in range(ranks)], me)
    for slot in range(ranks):
        array, entry = place(slot, ranks)
        low = lax.rem(peer_of(me, slot, ranks) + 8 * ranks - first, ranks)
        for k in range(capacity):
            block = low + k * ranks

            @pl.when(block < live)
            def _(array=array, entry=entry, k=k, block=block):
                patch_grad[block] = came[array][entry, k]

            @pl.when((block >= live) & (block < patch_grad.shape[0]))
            def _(block=block):
                patch_grad[block] = jnp.zeros(patch_grad.shape[1:], BF16)


def per_device(
    sizes,
    patches,
    unit_counts,
    segment_ids,
    merged_position,
    ln_gain,
    ln_bias,
    qkv_weight,
    out_weight,
    merge_gain,
    merge_bias,
    merged_grad,
):
    ranks, owners = sizes
    width = patches.shape[1]
    source_units = patches.shape[0] // UNIT
    rows = segment_ids.shape[0]
    capacity = -(-source_units // ranks)
    owner_slots, token_width = merged_grad.shape
    pair = owner_slots // owners
    inner = out_weight.shape[0]
    heads = inner // HEAD
    padded = -(-inner // LANES) * LANES
    counts = unit_counts.reshape(-1)
    smem = pl.BlockSpec(memory_space=pltpu.SMEM)
    vmem = pl.BlockSpec(memory_space=pltpu.VMEM)
    anywhere = pl.BlockSpec(memory_space=pl.ANY)

    block_shapes = pieces(ranks, (capacity, UNIT, width), BF16)
    beside = paired(ranks) and paired(owners) and pair == 8
    window_shape = jax.ShapeDtypeStruct(
        (owners, pair, token_width + (width if beside else 0)), BF16
    )
    n_in = len(block_shapes)
    swap = functools.partial(
        lax.all_to_all, axis_name="ctx", split_axis=0, concat_axis=0, tiled=True
    )

    outgoing = pl.pallas_call(
        functools.partial(pack_blocks, sizes, capacity),
        out_shape=block_shapes,
        in_specs=[smem, anywhere],
        out_specs=[vmem] * n_in,
        scratch_shapes=[pltpu.SemaphoreType.DMA((ranks * capacity,))],
        compiler_params=pltpu.CompilerParams(vmem_limit_bytes=4 * 2**20),
        name="pack_blocks",
    )(
        in_hbm(counts),
        in_hbm(patches.reshape(source_units, UNIT, width)),
    )
    arrived = exchange(outgoing, "dp", ranks)

    grad_blocks = merged_grad.reshape(owners, pair, token_width)
    grads = swap(grad_blocks)

    near = pl.pallas_call(
        hold,
        out_shape=pltpu.VMEM(qkv_weight.T.shape, BF16),
        in_specs=[anywhere],
        out_specs=vmem,
        scratch_shapes=[pltpu.SemaphoreType.DMA((HOLD_PARTS,))],
        compiler_params=pltpu.CompilerParams(vmem_limit_bytes=2**20),
        cost_estimate=pl.CostEstimate(flops=HOLD_FLOPS, bytes_accessed=10**6, transcendentals=0),
        name="hold",
    )(in_hbm(qkv_weight.T))

    wide = jax.ShapeDtypeStruct((rows, padded), BF16)
    state = pl.pallas_call(
        functools.partial(front_kernel, sizes, capacity),
        out_shape=[
            jax.ShapeDtypeStruct((rows, width), BF16),
            jax.ShapeDtypeStruct((rows, width), F32),
            jax.ShapeDtypeStruct((rows, LANES), F32),
            wide,
            wide,
            wide,
        ],
        in_specs=[smem] + [vmem] * (3 + n_in),
        out_specs=[vmem] * 6,
        compiler_params=pltpu.CompilerParams(vmem_limit_bytes=16 * 2**20),
        cost_estimate=pl.CostEstimate(
            flops=FRONT_FLOPS, bytes_accessed=8 * 10**6, transcendentals=0
        ),
        name="front",
    )(
        *map(in_hbm, (counts, ln_gain, ln_bias)),
        near,
        in_hbm(arrived[0]),
        *arrived[1:],
    )

    results = pl.pallas_call(
        functools.partial(block_kernel, sizes, capacity),
        out_shape=[
            *block_shapes,
            window_shape,
            jax.ShapeDtypeStruct((4, width), F32),
        ],
        in_specs=[smem] + [vmem] * 5 + [anywhere] * 2 + [vmem] * 7,
        out_specs=[vmem] * (n_in + 2),
        scratch_shapes=[
            pltpu.VMEM((rows, padded), F32),
            pltpu.VMEM((heads // 2, rows, 2 * rows), F32),
            pltpu.VMEM((rows, padded), F32),
            pltpu.VMEM((rows, padded), F32),
            pltpu.VMEM((rows, padded), F32),
            pltpu.VMEM((rows, padded), BF16),
            pltpu.VMEM((MERGE * owners * pair, width), F32),
            pltpu.VMEM((rows // UNIT, UNIT, width), BF16),
            pltpu.VMEM((4, width), F32),
            pltpu.VMEM((3 * inner, width), BF16),
            pltpu.VMEM((inner, width), BF16),
            pltpu.SemaphoreType.DMA((2,)),
        ],
        compiler_params=pltpu.CompilerParams(vmem_limit_bytes=40 * 2**20),
        cost_estimate=pl.CostEstimate(
            flops=2 * 10**9, bytes_accessed=12 * 10**6, transcendentals=200_000
        ),
        name="block",
    )(
        *map(
            in_hbm,
            (
                counts,
                segment_ids.reshape(1, rows),
                merged_position.reshape(1, rows // MERGE),
                ln_gain,
                merge_gain,
                merge_bias,
                qkv_weight.T,
                out_weight,
            ),
        ),
        *state,
        grads,
    )
    came_back = exchange(results[:n_in], "dp", ranks)
    merged = swap(results[n_in])
    patch_grad = pl.pallas_call(
        functools.partial(unpack_kernel, sizes, capacity),
        out_shape=jax.ShapeDtypeStruct((source_units, UNIT, width), BF16),
        in_specs=[smem] + [vmem] * n_in,
        out_specs=vmem,
        compiler_params=pltpu.CompilerParams(vmem_limit_bytes=8 * 2**20),
        cost_estimate=pl.CostEstimate(
            flops=UNPACK_FLOPS, bytes_accessed=10**6, transcendentals=0
        ),
        name="unpack",
    )(in_hbm(counts), in_hbm(came_back[0]), *came_back[1:])
    if beside:
        halves = merged[:, :, token_width:].astype(F32)
        terms = jnp.sum(halves[:, :4] + halves[:, 4:], axis=0)
        terms, patch_grad = lax.optimization_barrier((terms, patch_grad))
        norm_grads = spread(terms, "dp", ranks, range(1, ranks))
        merged = merged[:, :, :token_width]
    else:
        norm_grads = lax.psum(results[-1], ("dp", "ctx"))
    return (
        merged.reshape(owner_slots, token_width),
        patch_grad.reshape(source_units * UNIT, width),
        norm_grads,
    )


def solution(mesh):
    return jax.shard_map(
        functools.partial(per_device, (mesh.shape["dp"], mesh.shape["ctx"])),
        mesh=mesh,
        in_specs=(
            P(("dp", "ctx"), None),
            P("ctx", None),
            P(("dp", "ctx")),
            P(("dp", "ctx")),
            P(),
            P(),
            P(),
            P(),
            P(),
            P(),
            P(("dp", "ctx"), None),
        ),
        out_specs=(P(("dp", "ctx"), None), P(("dp", "ctx"), None), P()),
        check_vma=False,
    )
```

```python
import functools

import jax
import jax.numpy as jnp
from jax import lax
from jax.experimental import pallas as pl
from jax.experimental.pallas import tpu as pltpu
from jax.sharding import PartitionSpec as P

HEAD = 80
UNIT = 32
MERGE = 4
EPS = 1e-06
NEG = -1e30
LANES = 128
WIN = 256
F32 = jnp.float32
BF16 = jnp.bfloat16
FRONT_FLOPS = 12 * 10**9
HOLD_PARTS = 6
HOLD_FLOPS = 10**8
UNPACK_FLOPS = 10**10


def paired(size):
    return size <= 8 and size & (size - 1) == 0


def peer_of(index, slot, size):
    return index ^ slot if paired(size) else slot


def place(slot, size):
    return (slot, 0) if paired(size) else (0, slot)


def in_hbm(array):
    return pltpu.with_memory_space_constraint(array, pltpu.HBM)


def pieces(size, shape, dtype):
    if paired(size):
        return [pltpu.HBM((1, *shape), dtype)] + [
            jax.ShapeDtypeStruct((1, *shape), dtype)
        ] * (size - 1)
    return [jax.ShapeDtypeStruct((size, *shape), dtype)]


def exchange(arrays, axis, size):
    if paired(size):
        return [arrays[0]] + [
            lax.ppermute(arrays[slot], axis, [(i, i ^ slot) for i in range(size)])
            for slot in range(1, size)
        ]
    return [lax.all_to_all(arrays[0], axis, split_axis=0, concat_axis=0, tiled=True)]


def spread(terms, axis, size, slots):
    others = [
        lax.ppermute(terms, axis, [(i, i ^ slot) for i in range(size)]) for slot in slots
    ]
    for other in others:
        terms = terms + other
    return terms


def starts(counts, ranks):
    out = [jnp.int32(0)]
    for rank in range(ranks - 1):
        out.append(out[-1] + counts[rank])
    return out


def chosen(values, index):
    out = values[0]
    for i in range(1, len(values)):
        out = jnp.where(index == i, values[i], out)
    return out


def pack_blocks(sizes, capacity, slots, counts, source, *rest):
    ranks = sizes[0]
    outs, sems = rest[:-1], rest[-1]
    me = lax.axis_index("dp")
    first = chosen(starts(counts, ranks), me)
    copies = []
    for i, slot in enumerate(slots):
        array, entry = (i, 0) if paired(ranks) else (0, slot)
        lead = lax.rem(peer_of(me, slot, ranks) + 8 * ranks - first, ranks)
        for k in range(capacity):
            block = jnp.minimum(lead + k * ranks, source.shape[0] - 1)
            copies.append(
                pltpu.make_async_copy(
                    source.at[block], outs[array].at[entry, k], sems.at[i * capacity + k]
                )
            )
            copies[-1].start()
    for copy in copies:
        copy.wait()


def hold(far, near, sems):
    count = sems.shape[0]
    step = far.shape[0] // count
    spans = [slice(i * step, (i + 1) * step) for i in range(count)]
    copies = [
        pltpu.make_async_copy(far.at[span], near.at[span], sems.at[i])
        for i, span in enumerate(spans)
    ]
    for copy in copies:
        copy.start()
    for copy in copies:
        copy.wait()


def moments(values):
    average = jnp.mean(values, axis=-1, keepdims=True)
    centred = values - average
    inverse = lax.rsqrt(jnp.mean(centred * centred, axis=-1, keepdims=True) + EPS)
    return centred * inverse, inverse


def norm_back(scaled, normed, inverse):
    centre = jnp.mean(scaled, axis=-1, keepdims=True)
    slope = jnp.mean(scaled * normed, axis=-1, keepdims=True)
    return inverse * (scaled - centre - normed * slope)


def dot(a, b, ca=1, cb=0):
    return lax.dot_general(a, b, (((ca,), (cb,)), ((), ())), preferred_element_type=F32)


def iota(shape, dim):
    return lax.broadcasted_iota(jnp.int32, shape, dim)


def front_kernel(sizes, capacity, *refs):
    ranks = sizes[0]
    n_in = ranks if paired(ranks) else 1
    counts, ln_gain, ln_bias, wq = refs[:4]
    arrived, refs = refs[4 : 4 + n_in], refs[4 + n_in :]
    xs, normed_ref, inverse_ref, qs, ks, vs = refs
    rows, width = xs.shape
    units = rows // UNIT
    inner = wq.shape[0] // 3
    thirds = [slice(part * inner, (part + 1) * inner) for part in range(3)]
    me = lax.axis_index("dp")
    begin = starts(counts, ranks)
    for unit in range(units):
        wanted = unit * ranks + me
        sender = jnp.int32(0)
        for rank in range(1, ranks):
            sender = jnp.where(begin[rank] <= wanted, rank, sender)
        kth = (wanted - chosen(begin, sender)) // ranks
        span = slice(unit * UNIT, (unit + 1) * UNIT)
        if n_in == 1:
            xs[span, :] = arrived[0][sender, kth]
        else:
            slot = sender ^ me
            value = arrived[0][0, kth]
            for i in range(1, n_in):
                value = jnp.where(slot == i, arrived[i][0, kth], value)
            xs[span, :] = value
    normed, inverse = moments(xs[...].astype(F32))
    normed_ref[...] = normed
    inverse_ref[...] = jnp.broadcast_to(inverse, inverse_ref.shape)
    gain, bias = ln_gain[...].reshape(1, width), ln_bias[...].reshape(1, width)
    shifted = (normed * gain + bias).astype(BF16)
    for ref, part in ((qs, 0), (ks, 1), (vs, 2)):
        ref[:, inner:] = jnp.zeros((rows, ref.shape[1] - inner), BF16)
        ref[:, :inner] = dot(shifted, wq[thirds[part], :], 1, 1).astype(BF16)


def block_kernel(sizes, capacity, *refs):
    ranks, owners = sizes
    n_in = ranks if paired(ranks) else 1
    counts, labels, positions, *params, wq_far, wo_far = refs[:8]
    xs, normed_ref, inverse_ref, qs, ks, vs, grads = refs[8:15]
    refs = refs[15:]
    back, refs = refs[:n_in], refs[n_in:]
    windows, terms_out, ats, ps, dqs, dks, dvs, gs, ws, rows_out, terms, wq, wo, sems = refs
    rows, width = xs.shape
    ln_gain, merge_gain, merge_bias = (ref[...].reshape(1, width) for ref in params)
    units = rows // UNIT
    inner = wo.shape[0]
    heads = inner // HEAD
    scale = HEAD ** (-0.5)
    tokens = rows // MERGE
    load_out = pltpu.make_async_copy(wo_far, wo, sems.at[0])
    load_qkv = pltpu.make_async_copy(wq_far, wq, sems.at[1])
    load_out.start()
    load_qkv.start()
    pair = grads.shape[1]
    slots = owners * pair
    me, column = lax.axis_index("dp"), lax.axis_index("ctx")
    begin = starts(counts, ranks)
    normed_in, inverse_in = normed_ref[...], inverse_ref[:, :1]

    label = jnp.broadcast_to(labels[...].astype(F32), (rows, rows))
    joined = (label == label.T) & (
        iota((rows, rows), 0) // UNIT == iota((rows, rows), 1) // UNIT
    )
    own = iota((rows, tokens), 0) // MERGE == iota((rows, tokens), 1)
    place_of = positions[...] - column * slots
    spot = jnp.sum(jnp.where(own, place_of.astype(F32), 0.0), axis=1, keepdims=True)
    spot_row = jnp.broadcast_to(spot, (rows, LANES)).T[:1, :]
    spot = spot.astype(jnp.int32)
    spot_row = spot_row.astype(jnp.int32)

    def slot_place(index):
        local = index % slots
        return (local % pair) * owners + local // pair

    lane = iota((rows, MERGE * slots), 1)
    take = (
        (iota((rows, MERGE * slots), 0) % MERGE == lane // slots) & (slot_place(lane) == spot)
    ).astype(BF16)
    lead = iota((MERGE * slots, rows), 0)
    put = (
        (iota((MERGE * slots, rows), 1) % MERGE == lead // slots) & (slot_place(lead) == spot_row)
    ).astype(BF16)

    zero = jnp.zeros((rows, gs.shape[1] - inner), BF16)
    ats[...] = jnp.zeros_like(ats)
    dqs[...] = jnp.zeros_like(dqs)
    dks[...] = jnp.zeros_like(dks)
    dvs[...] = jnp.zeros_like(dvs)

    win_lane = iota((rows, WIN), 1)
    none = jnp.zeros((), BF16)

    def window(two):
        at = 2 * two * HEAD
        low = at // LANES * LANES
        first = (win_lane >= at - low) & (win_lane < at - low + HEAD)
        second = (win_lane >= at - low + HEAD) & (win_lane < at - low + 2 * HEAD)
        return slice(low, low + WIN), first, second

    def stacked(value, first, second):
        return jnp.concatenate(
            [jnp.where(first, value, none), jnp.where(second, value, none)], axis=0
        )

    def own_part(value, first, second):
        return jnp.where(first, value[:rows], jnp.where(second, value[rows:], 0.0))

    for two in range(heads // 2):
        span, first, second = window(two)
        scores = dot(qs[:, span], stacked(ks[:, span], first, second), 1, 1) * scale
        for side in range(2):
            half = slice(side * rows, (side + 1) * rows)
            score = jnp.where(joined, scores[:, half], NEG)
            raised = jnp.exp(score - jnp.max(score, axis=-1, keepdims=True))
            ps[two, :, half] = raised / jnp.sum(raised, axis=-1, keepdims=True)
        ats[:, span] += dot(ps[two].astype(BF16), stacked(vs[:, span], first, second))
    load_out.wait()
    hidden = xs[...].astype(F32) + dot(ats[:, :inner].astype(BF16), wo[...])
    normed_out, inverse_out = moments(hidden)
    result = (normed_out * merge_gain + merge_bias).astype(BF16)
    ws[...] = dot(put, result)
    for owner in range(owners):
        for part in range(MERGE):
            start = part * slots + owner * pair
            windows[owner, :, part * width : (part + 1) * width] = ws[
                start : start + pair, :
            ].astype(BF16)

    for owner in range(owners):
        for part in range(MERGE):
            start = part * slots + owner * pair
            ws[start : start + pair, :] = grads[
                owner, :, part * width : (part + 1) * width
            ].astype(F32)
    upstream = dot(take, ws[...].astype(BF16))
    terms[2:3, :] = jnp.sum(upstream * normed_out, axis=0, keepdims=True)
    terms[3:4, :] = jnp.sum(upstream, axis=0, keepdims=True)
    hidden_grad = norm_back(upstream * merge_gain, normed_out, inverse_out)
    gs[:, :inner] = dot(hidden_grad.astype(BF16), wo[...], 1, 1).astype(BF16)
    gs[:, inner:] = zero
    for two in range(heads // 2):
        span, first, second = window(two)
        prob = ps[two]
        grad = gs[:, span]
        prob_grad = dot(grad, stacked(vs[:, span], first, second), 1, 1)
        dvs[:, span] += own_part(dot(prob.astype(BF16), grad, 0, 0), first, second)
        weighted = prob * prob_grad
        centred = [
            prob_grad[:, half] - jnp.sum(weighted[:, half], axis=-1, keepdims=True)
            for half in (slice(0, rows), slice(rows, 2 * rows))
        ]
        score_grad = (prob * jnp.concatenate(centred, axis=1) * scale).astype(BF16)
        dqs[:, span] += dot(score_grad, stacked(ks[:, span], first, second))
        dks[:, span] += own_part(dot(score_grad, qs[:, span], 0, 0), first, second)
    load_qkv.wait()
    input_grad = sum(
        dot(ref[:, :inner].astype(BF16), wq[part * inner : (part + 1) * inner, :])
        for ref, part in ((dqs, 0), (dks, 1), (dvs, 2))
    )
    terms[0:1, :] = jnp.sum(input_grad * normed_in, axis=0, keepdims=True)
    terms[1:2, :] = jnp.sum(input_grad, axis=0, keepdims=True)
    row_grad = hidden_grad + norm_back(input_grad * ln_gain, normed_in, inverse_in)
    rows_out[...] = row_grad.astype(BF16).reshape(units, UNIT, width)

    terms_out[...] = terms[...]
    spare = windows.shape[2] - MERGE * width
    if spare:
        high = terms[...].astype(BF16)
        low = (terms[...] - high.astype(F32)).astype(BF16)
        for owner in range(owners):
            windows[owner, :, MERGE * width :] = jnp.concatenate([high, low], axis=0)

    for slot in range(ranks):
        array, entry = place(slot, ranks)
        peer = peer_of(me, slot, ranks)
        base_of = chosen(begin, peer)
        low = lax.rem(me + 8 * ranks - base_of, ranks)
        for k in range(capacity):
            unit = jnp.minimum((base_of + low + k * ranks) // ranks, units - 1)
            back[array][entry, k] = rows_out[unit]


def unpack_kernel(sizes, capacity, *refs):
    ranks = sizes[0]
    counts, *came, patch_grad = refs
    me = lax.axis_index("dp")
    first = chosen(starts(counts, ranks), me)
    live = chosen([counts[rank] for rank in range(ranks)], me)
    for slot in range(ranks):
        array, entry = place(slot, ranks)
        low = lax.rem(peer_of(me, slot, ranks) + 8 * ranks - first, ranks)
        for k in range(capacity):
            block = low + k * ranks

            @pl.when(block < live)
            def _(array=array, entry=entry, k=k, block=block):
                patch_grad[block] = came[array][entry, k]

            @pl.when((block >= live) & (block < patch_grad.shape[0]))
            def _(block=block):
                patch_grad[block] = jnp.zeros(patch_grad.shape[1:], BF16)


def per_device(
    sizes,
    patches,
    unit_counts,
    segment_ids,
    merged_position,
    ln_gain,
    ln_bias,
    qkv_weight,
    out_weight,
    merge_gain,
    merge_bias,
    merged_grad,
):
    ranks, owners = sizes
    width = patches.shape[1]
    source_units = patches.shape[0] // UNIT
    rows = segment_ids.shape[0]
    capacity = -(-source_units // ranks)
    owner_slots, token_width = merged_grad.shape
    pair = owner_slots // owners
    inner = out_weight.shape[0]
    heads = inner // HEAD
    padded = -(-inner // LANES) * LANES
    counts = unit_counts.reshape(-1)
    smem = pl.BlockSpec(memory_space=pltpu.SMEM)
    vmem = pl.BlockSpec(memory_space=pltpu.VMEM)
    anywhere = pl.BlockSpec(memory_space=pl.ANY)

    block_shapes = pieces(ranks, (capacity, UNIT, width), BF16)
    beside = paired(ranks) and paired(owners) and pair == 8
    window_shape = jax.ShapeDtypeStruct(
        (owners, pair, token_width + (width if beside else 0)), BF16
    )
    n_in = len(block_shapes)
    swap = functools.partial(
        lax.all_to_all, axis_name="ctx", split_axis=0, concat_axis=0, tiled=True
    )

    def packed(slots, shapes, name):
        return pl.pallas_call(
            functools.partial(pack_blocks, sizes, capacity, slots),
            out_shape=shapes,
            in_specs=[smem, anywhere],
            out_specs=[vmem] * len(shapes),
            scratch_shapes=[pltpu.SemaphoreType.DMA((len(slots) * capacity,))],
            compiler_params=pltpu.CompilerParams(vmem_limit_bytes=4 * 2**20),
            name=name,
        )(in_hbm(counts), in_hbm(patches.reshape(source_units, UNIT, width)))

    if paired(ranks):
        outgoing = [
            *packed([0], block_shapes[:1], "pack_own"),
            *packed(range(1, ranks), block_shapes[1:], "pack_blocks"),
        ]
    else:
        outgoing = packed(range(ranks), block_shapes, "pack_blocks")
    arrived = exchange(outgoing, "dp", ranks)

    grad_blocks = merged_grad.reshape(owners, pair, token_width)
    grads = swap(grad_blocks)

    near = pl.pallas_call(
        hold,
        out_shape=pltpu.VMEM(qkv_weight.T.shape, BF16),
        in_specs=[anywhere],
        out_specs=vmem,
        scratch_shapes=[pltpu.SemaphoreType.DMA((HOLD_PARTS,))],
        compiler_params=pltpu.CompilerParams(vmem_limit_bytes=2**20),
        cost_estimate=pl.CostEstimate(flops=HOLD_FLOPS, bytes_accessed=10**6, transcendentals=0),
        name="hold",
    )(in_hbm(qkv_weight.T))

    wide = jax.ShapeDtypeStruct((rows, padded), BF16)
    state = pl.pallas_call(
        functools.partial(front_kernel, sizes, capacity),
        out_shape=[
            jax.ShapeDtypeStruct((rows, width), BF16),
            jax.ShapeDtypeStruct((rows, width), F32),
            jax.ShapeDtypeStruct((rows, LANES), F32),
            wide,
            wide,
            wide,
        ],
        in_specs=[smem] + [vmem] * (3 + n_in),
        out_specs=[vmem] * 6,
        compiler_params=pltpu.CompilerParams(vmem_limit_bytes=16 * 2**20),
        cost_estimate=pl.CostEstimate(
            flops=FRONT_FLOPS, bytes_accessed=8 * 10**6, transcendentals=0
        ),
        name="front",
    )(
        *map(in_hbm, (counts, ln_gain, ln_bias)),
        near,
        in_hbm(arrived[0]),
        *arrived[1:],
    )

    results = pl.pallas_call(
        functools.partial(block_kernel, sizes, capacity),
        out_shape=[
            *block_shapes,
            window_shape,
            jax.ShapeDtypeStruct((4, width), F32),
        ],
        in_specs=[smem] + [vmem] * 5 + [anywhere] * 2 + [vmem] * 7,
        out_specs=[vmem] * (n_in + 2),
        scratch_shapes=[
            pltpu.VMEM((rows, padded), F32),
            pltpu.VMEM((heads // 2, rows, 2 * rows), F32),
            pltpu.VMEM((rows, padded), F32),
            pltpu.VMEM((rows, padded), F32),
            pltpu.VMEM((rows, padded), F32),
            pltpu.VMEM((rows, padded), BF16),
            pltpu.VMEM((MERGE * owners * pair, width), F32),
            pltpu.VMEM((rows // UNIT, UNIT, width), BF16),
            pltpu.VMEM((4, width), F32),
            pltpu.VMEM((3 * inner, width), BF16),
            pltpu.VMEM((inner, width), BF16),
            pltpu.SemaphoreType.DMA((2,)),
        ],
        compiler_params=pltpu.CompilerParams(vmem_limit_bytes=40 * 2**20),
        cost_estimate=pl.CostEstimate(
            flops=2 * 10**9, bytes_accessed=12 * 10**6, transcendentals=200_000
        ),
        name="block",
    )(
        *map(
            in_hbm,
            (
                counts,
                segment_ids.reshape(1, rows),
                merged_position.reshape(1, rows // MERGE),
                ln_gain,
                merge_gain,
                merge_bias,
                qkv_weight.T,
                out_weight,
            ),
        ),
        *state,
        grads,
    )
    came_back = exchange(results[:n_in], "dp", ranks)
    merged = swap(results[n_in])
    patch_grad = pl.pallas_call(
        functools.partial(unpack_kernel, sizes, capacity),
        out_shape=jax.ShapeDtypeStruct((source_units, UNIT, width), BF16),
        in_specs=[smem] + [vmem] * n_in,
        out_specs=vmem,
        compiler_params=pltpu.CompilerParams(vmem_limit_bytes=8 * 2**20),
        cost_estimate=pl.CostEstimate(
            flops=UNPACK_FLOPS, bytes_accessed=10**6, transcendentals=0
        ),
        name="unpack",
    )(in_hbm(counts), in_hbm(came_back[0]), *came_back[1:])
    if beside:
        halves = merged[:, :, token_width:].astype(F32)
        terms = jnp.sum(halves[:, :4] + halves[:, 4:], axis=0)
        terms, patch_grad = lax.optimization_barrier((terms, patch_grad))
        norm_grads = spread(terms, "dp", ranks, range(1, ranks))
        merged = merged[:, :, :token_width]
    else:
        norm_grads = lax.psum(results[-1], ("dp", "ctx"))
    return (
        merged.reshape(owner_slots, token_width),
        patch_grad.reshape(source_units * UNIT, width),
        norm_grads,
    )


def solution(mesh):
    return jax.shard_map(
        functools.partial(per_device, (mesh.shape["dp"], mesh.shape["ctx"])),
        mesh=mesh,
        in_specs=(
            P(("dp", "ctx"), None),
            P("ctx", None),
            P(("dp", "ctx")),
            P(("dp", "ctx")),
            P(),
            P(),
            P(),
            P(),
            P(),
            P(),
            P(("dp", "ctx"), None),
        ),
        out_specs=(P(("dp", "ctx"), None), P(("dp", "ctx"), None), P()),
        check_vma=False,
    )
```

```python
import functools

import jax
import jax.numpy as jnp
from jax import lax
from jax.experimental import pallas as pl
from jax.experimental.pallas import tpu as pltpu
from jax.sharding import PartitionSpec as P

HEAD = 80
UNIT = 32
MERGE = 4
EPS = 1e-06
NEG = -1e30
LANES = 128
WIN = 256
F32 = jnp.float32
BF16 = jnp.bfloat16
FRONT_FLOPS = 12 * 10**9
HOLD_PARTS = 6
HOLD_FLOPS = 10**8
UNPACK_FLOPS = 10**10


def paired(size):
    return size <= 8 and size & (size - 1) == 0


def peer_of(index, slot, size):
    return index ^ slot if paired(size) else slot


def place(slot, size):
    return (slot, 0) if paired(size) else (0, slot)


def in_hbm(array):
    return pltpu.with_memory_space_constraint(array, pltpu.HBM)


def pieces(size, shape, dtype):
    if paired(size):
        return [pltpu.HBM((1, *shape), dtype)] + [
            jax.ShapeDtypeStruct((1, *shape), dtype)
        ] * (size - 1)
    return [jax.ShapeDtypeStruct((size, *shape), dtype)]


def exchange(arrays, axis, size):
    if paired(size):
        return [arrays[0]] + [
            lax.ppermute(arrays[slot], axis, [(i, i ^ slot) for i in range(size)])
            for slot in range(1, size)
        ]
    return [lax.all_to_all(arrays[0], axis, split_axis=0, concat_axis=0, tiled=True)]


def spread(terms, axis, size, slots):
    others = [
        lax.ppermute(terms, axis, [(i, i ^ slot) for i in range(size)]) for slot in slots
    ]
    for other in others:
        terms = terms + other
    return terms


def starts(counts, ranks):
    out = [jnp.int32(0)]
    for rank in range(ranks - 1):
        out.append(out[-1] + counts[rank])
    return out


def chosen(values, index):
    out = values[0]
    for i in range(1, len(values)):
        out = jnp.where(index == i, values[i], out)
    return out


def pack_blocks(sizes, capacity, slots, counts, source, *rest):
    ranks = sizes[0]
    outs, sems = rest[:-1], rest[-1]
    me = lax.axis_index("dp")
    first = chosen(starts(counts, ranks), me)
    copies = []
    for i, slot in enumerate(slots):
        array, entry = (i, 0) if paired(ranks) else (0, slot)
        lead = lax.rem(peer_of(me, slot, ranks) + 8 * ranks - first, ranks)
        for k in range(capacity):
            block = jnp.minimum(lead + k * ranks, source.shape[0] - 1)
            copies.append(
                pltpu.make_async_copy(
                    source.at[block], outs[array].at[entry, k], sems.at[i * capacity + k]
                )
            )
            copies[-1].start()
    for copy in copies:
        copy.wait()


def hold(far, near, sems):
    count = sems.shape[0]
    step = far.shape[0] // count
    spans = [slice(i * step, (i + 1) * step) for i in range(count)]
    copies = [
        pltpu.make_async_copy(far.at[span], near.at[span], sems.at[i])
        for i, span in enumerate(spans)
    ]
    for copy in copies:
        copy.start()
    for copy in copies:
        copy.wait()


def moments(values):
    average = jnp.mean(values, axis=-1, keepdims=True)
    centred = values - average
    inverse = lax.rsqrt(jnp.mean(centred * centred, axis=-1, keepdims=True) + EPS)
    return centred * inverse, inverse


def norm_back(scaled, normed, inverse):
    centre = jnp.mean(scaled, axis=-1, keepdims=True)
    slope = jnp.mean(scaled * normed, axis=-1, keepdims=True)
    return inverse * (scaled - centre - normed * slope)


def dot(a, b, ca=1, cb=0):
    return lax.dot_general(a, b, (((ca,), (cb,)), ((), ())), preferred_element_type=F32)


def iota(shape, dim):
    return lax.broadcasted_iota(jnp.int32, shape, dim)


def front_kernel(sizes, capacity, *refs):
    ranks = sizes[0]
    n_in = ranks if paired(ranks) else 1
    counts, ln_gain, ln_bias, wq = refs[:4]
    arrived, refs = refs[4 : 4 + n_in], refs[4 + n_in :]
    xs, normed_ref, inverse_ref, qs, ks, vs = refs
    rows, width = xs.shape
    units = rows // UNIT
    inner = wq.shape[0] // 3
    thirds = [slice(part * inner, (part + 1) * inner) for part in range(3)]
    me = lax.axis_index("dp")
    begin = starts(counts, ranks)
    for unit in range(units):
        wanted = unit * ranks + me
        sender = jnp.int32(0)
        for rank in range(1, ranks):
            sender = jnp.where(begin[rank] <= wanted, rank, sender)
        kth = (wanted - chosen(begin, sender)) // ranks
        span = slice(unit * UNIT, (unit + 1) * UNIT)
        if n_in == 1:
            xs[span, :] = arrived[0][sender, kth]
        else:
            slot = sender ^ me
            value = arrived[0][0, kth]
            for i in range(1, n_in):
                value = jnp.where(slot == i, arrived[i][0, kth], value)
            xs[span, :] = value
    normed, inverse = moments(xs[...].astype(F32))
    normed_ref[...] = normed
    inverse_ref[...] = jnp.broadcast_to(inverse, inverse_ref.shape)
    gain, bias = ln_gain[...].reshape(1, width), ln_bias[...].reshape(1, width)
    shifted = (normed * gain + bias).astype(BF16)
    for ref, part in ((qs, 0), (ks, 1), (vs, 2)):
        ref[:, inner:] = jnp.zeros((rows, ref.shape[1] - inner), BF16)
        ref[:, :inner] = dot(shifted, wq[thirds[part], :], 1, 1).astype(BF16)


def block_kernel(sizes, capacity, *refs):
    ranks, owners = sizes
    n_in = ranks if paired(ranks) else 1
    counts, labels, positions, *params, wq_far, wo_far = refs[:8]
    xs, normed_ref, inverse_ref, qs, ks, vs, grads = refs[8:15]
    refs = refs[15:]
    back, refs = refs[:n_in], refs[n_in:]
    windows, terms_out, ats, ps, dqs, dks, dvs, gs, ws, rows_out, terms, wq, wo, sems = refs
    rows, width = xs.shape
    ln_gain, merge_gain, merge_bias = (ref[...].reshape(1, width) for ref in params)
    units = rows // UNIT
    inner = wo.shape[0]
    heads = inner // HEAD
    scale = HEAD ** (-0.5)
    tokens = rows // MERGE
    load_out = pltpu.make_async_copy(wo_far, wo, sems.at[0])
    load_qkv = pltpu.make_async_copy(wq_far, wq, sems.at[1])
    load_out.start()
    load_qkv.start()
    pair = grads.shape[1]
    slots = owners * pair
    me, column = lax.axis_index("dp"), lax.axis_index("ctx")
    begin = starts(counts, ranks)
    normed_in, inverse_in = normed_ref[...], inverse_ref[:, :1]

    label = jnp.broadcast_to(labels[...].astype(F32), (rows, rows))
    joined = (label == label.T) & (
        iota((rows, rows), 0) // UNIT == iota((rows, rows), 1) // UNIT
    )
    own = iota((rows, tokens), 0) // MERGE == iota((rows, tokens), 1)
    place_of = positions[...] - column * slots
    spot = jnp.sum(jnp.where(own, place_of.astype(F32), 0.0), axis=1, keepdims=True)
    spot_row = jnp.broadcast_to(spot, (rows, LANES)).T[:1, :]
    spot = spot.astype(jnp.int32)
    spot_row = spot_row.astype(jnp.int32)

    def slot_place(index):
        local = index % slots
        return (local % pair) * owners + local // pair

    lane = iota((rows, MERGE * slots), 1)
    take = (
        (iota((rows, MERGE * slots), 0) % MERGE == lane // slots) & (slot_place(lane) == spot)
    ).astype(BF16)
    lead = iota((MERGE * slots, rows), 0)
    put = (
        (iota((MERGE * slots, rows), 1) % MERGE == lead // slots) & (slot_place(lead) == spot_row)
    ).astype(BF16)

    zero = jnp.zeros((rows, gs.shape[1] - inner), BF16)
    ats[...] = jnp.zeros_like(ats)
    dqs[...] = jnp.zeros_like(dqs)
    dks[...] = jnp.zeros_like(dks)
    dvs[...] = jnp.zeros_like(dvs)

    win_lane = iota((rows, WIN), 1)
    none = jnp.zeros((), BF16)

    def window(two):
        at = 2 * two * HEAD
        low = at // LANES * LANES
        first = (win_lane >= at - low) & (win_lane < at - low + HEAD)
        second = (win_lane >= at - low + HEAD) & (win_lane < at - low + 2 * HEAD)
        return slice(low, low + WIN), first, second

    def stacked(value, first, second):
        return jnp.concatenate(
            [jnp.where(first, value, none), jnp.where(second, value, none)], axis=0
        )

    def own_part(value, first, second):
        return jnp.where(first, value[:rows], jnp.where(second, value[rows:], 0.0))

    for two in range(heads // 2):
        span, first, second = window(two)
        scores = dot(qs[:, span], stacked(ks[:, span], first, second), 1, 1) * scale
        for side in range(2):
            half = slice(side * rows, (side + 1) * rows)
            score = jnp.where(joined, scores[:, half], NEG)
            raised = jnp.exp(score - jnp.max(score, axis=-1, keepdims=True))
            ps[two, :, half] = raised / jnp.sum(raised, axis=-1, keepdims=True)
        ats[:, span] += dot(ps[two].astype(BF16), stacked(vs[:, span], first, second))
    load_out.wait()
    hidden = xs[...].astype(F32) + dot(ats[:, :inner].astype(BF16), wo[...])
    normed_out, inverse_out = moments(hidden)
    result = (normed_out * merge_gain + merge_bias).astype(BF16)
    ws[...] = dot(put, result)
    for owner in range(owners):
        for part in range(MERGE):
            start = part * slots + owner * pair
            windows[owner, :, part * width : (part + 1) * width] = ws[
                start : start + pair, :
            ].astype(BF16)

    for owner in range(owners):
        for part in range(MERGE):
            start = part * slots + owner * pair
            ws[start : start + pair, :] = grads[
                owner, :, part * width : (part + 1) * width
            ].astype(F32)
    upstream = dot(take, ws[...].astype(BF16))
    terms[2:3, :] = jnp.sum(upstream * normed_out, axis=0, keepdims=True)
    terms[3:4, :] = jnp.sum(upstream, axis=0, keepdims=True)
    hidden_grad = norm_back(upstream * merge_gain, normed_out, inverse_out)
    gs[:, :inner] = dot(hidden_grad.astype(BF16), wo[...], 1, 1).astype(BF16)
    gs[:, inner:] = zero
    for two in range(heads // 2):
        span, first, second = window(two)
        prob = ps[two]
        grad = gs[:, span]
        prob_grad = dot(grad, stacked(vs[:, span], first, second), 1, 1)
        dvs[:, span] += own_part(dot(prob.astype(BF16), grad, 0, 0), first, second)
        weighted = prob * prob_grad
        centred = [
            prob_grad[:, half] - jnp.sum(weighted[:, half], axis=-1, keepdims=True)
            for half in (slice(0, rows), slice(rows, 2 * rows))
        ]
        score_grad = (prob * jnp.concatenate(centred, axis=1) * scale).astype(BF16)
        dqs[:, span] += dot(score_grad, stacked(ks[:, span], first, second))
        dks[:, span] += own_part(dot(score_grad, qs[:, span], 0, 0), first, second)
    load_qkv.wait()
    input_grad = sum(
        dot(ref[:, :inner].astype(BF16), wq[part * inner : (part + 1) * inner, :])
        for ref, part in ((dqs, 0), (dks, 1), (dvs, 2))
    )
    terms[0:1, :] = jnp.sum(input_grad * normed_in, axis=0, keepdims=True)
    terms[1:2, :] = jnp.sum(input_grad, axis=0, keepdims=True)
    row_grad = hidden_grad + norm_back(input_grad * ln_gain, normed_in, inverse_in)
    rows_out[...] = row_grad.astype(BF16).reshape(units, UNIT, width)

    terms_out[...] = terms[...]
    spare = windows.shape[2] - MERGE * width
    if spare:
        high = terms[...].astype(BF16)
        low = (terms[...] - high.astype(F32)).astype(BF16)
        for owner in range(owners):
            windows[owner, :, MERGE * width :] = jnp.concatenate([high, low], axis=0)

    for slot in range(ranks):
        array, entry = place(slot, ranks)
        peer = peer_of(me, slot, ranks)
        base_of = chosen(begin, peer)
        low = lax.rem(me + 8 * ranks - base_of, ranks)
        for k in range(capacity):
            unit = jnp.minimum((base_of + low + k * ranks) // ranks, units - 1)
            back[array][entry, k] = rows_out[unit]


def unpack_kernel(sizes, capacity, *refs):
    ranks = sizes[0]
    counts, *came, patch_grad = refs
    me = lax.axis_index("dp")
    first = chosen(starts(counts, ranks), me)
    live = chosen([counts[rank] for rank in range(ranks)], me)
    for slot in range(ranks):
        array, entry = place(slot, ranks)
        low = lax.rem(peer_of(me, slot, ranks) + 8 * ranks - first, ranks)
        for k in range(capacity):
            block = low + k * ranks

            @pl.when(block < live)
            def _(array=array, entry=entry, k=k, block=block):
                patch_grad[block] = came[array][entry, k]

            @pl.when((block >= live) & (block < patch_grad.shape[0]))
            def _(block=block):
                patch_grad[block] = jnp.zeros(patch_grad.shape[1:], BF16)


def per_device(
    sizes,
    patches,
    unit_counts,
    segment_ids,
    merged_position,
    ln_gain,
    ln_bias,
    qkv_weight,
    out_weight,
    merge_gain,
    merge_bias,
    merged_grad,
):
    ranks, owners = sizes
    width = patches.shape[1]
    source_units = patches.shape[0] // UNIT
    rows = segment_ids.shape[0]
    capacity = -(-source_units // ranks)
    owner_slots, token_width = merged_grad.shape
    pair = owner_slots // owners
    inner = out_weight.shape[0]
    heads = inner // HEAD
    padded = -(-inner // LANES) * LANES
    counts = unit_counts.reshape(-1)
    smem = pl.BlockSpec(memory_space=pltpu.SMEM)
    vmem = pl.BlockSpec(memory_space=pltpu.VMEM)
    anywhere = pl.BlockSpec(memory_space=pl.ANY)

    block_shapes = pieces(ranks, (capacity, UNIT, width), BF16)
    beside = paired(ranks) and paired(owners) and pair == 8
    window_shape = jax.ShapeDtypeStruct(
        (owners, pair, token_width + (width if beside else 0)), BF16
    )
    n_in = len(block_shapes)
    swap = functools.partial(
        lax.all_to_all, axis_name="ctx", split_axis=0, concat_axis=0, tiled=True
    )

    def packed(slots, shapes, name):
        return pl.pallas_call(
            functools.partial(pack_blocks, sizes, capacity, slots),
            out_shape=shapes,
            in_specs=[smem, anywhere],
            out_specs=[vmem] * len(shapes),
            scratch_shapes=[pltpu.SemaphoreType.DMA((len(slots) * capacity,))],
            compiler_params=pltpu.CompilerParams(vmem_limit_bytes=4 * 2**20),
            name=name,
        )(in_hbm(counts), in_hbm(patches.reshape(source_units, UNIT, width)))

    if paired(ranks):
        outgoing = [
            *packed([0], block_shapes[:1], "pack_own"),
            *packed(range(1, ranks), block_shapes[1:], "pack_blocks"),
        ]
    else:
        outgoing = packed(range(ranks), block_shapes, "pack_blocks")
    arrived = exchange(outgoing, "dp", ranks)

    grad_blocks = merged_grad.reshape(owners, pair, token_width)
    grads = swap(grad_blocks)

    near = pl.pallas_call(
        hold,
        out_shape=pltpu.VMEM(qkv_weight.T.shape, BF16),
        in_specs=[anywhere],
        out_specs=vmem,
        scratch_shapes=[pltpu.SemaphoreType.DMA((HOLD_PARTS,))],
        compiler_params=pltpu.CompilerParams(vmem_limit_bytes=2**20),
        cost_estimate=pl.CostEstimate(flops=HOLD_FLOPS, bytes_accessed=10**6, transcendentals=0),
        name="hold",
    )(in_hbm(qkv_weight.T))

    wide = jax.ShapeDtypeStruct((rows, padded), BF16)
    state = pl.pallas_call(
        functools.partial(front_kernel, sizes, capacity),
        out_shape=[
            jax.ShapeDtypeStruct((rows, width), BF16),
            jax.ShapeDtypeStruct((rows, width), F32),
            jax.ShapeDtypeStruct((rows, LANES), F32),
            wide,
            wide,
            wide,
        ],
        in_specs=[smem] + [vmem] * (3 + n_in),
        out_specs=[vmem] * 6,
        compiler_params=pltpu.CompilerParams(vmem_limit_bytes=16 * 2**20),
        cost_estimate=pl.CostEstimate(
            flops=FRONT_FLOPS, bytes_accessed=8 * 10**6, transcendentals=0
        ),
        name="front",
    )(
        *map(in_hbm, (counts, ln_gain, ln_bias)),
        near,
        in_hbm(arrived[0]),
        *arrived[1:],
    )

    results = pl.pallas_call(
        functools.partial(block_kernel, sizes, capacity),
        out_shape=[
            *block_shapes,
            window_shape,
            jax.ShapeDtypeStruct((4, width), F32),
        ],
        in_specs=[smem] + [vmem] * 5 + [anywhere] * 2 + [vmem] * 7,
        out_specs=[vmem] * (n_in + 2),
        scratch_shapes=[
            pltpu.VMEM((rows, padded), F32),
            pltpu.VMEM((heads // 2, rows, 2 * rows), F32),
            pltpu.VMEM((rows, padded), F32),
            pltpu.VMEM((rows, padded), F32),
            pltpu.VMEM((rows, padded), F32),
            pltpu.VMEM((rows, padded), BF16),
            pltpu.VMEM((MERGE * owners * pair, width), F32),
            pltpu.VMEM((rows // UNIT, UNIT, width), BF16),
            pltpu.VMEM((4, width), F32),
            pltpu.VMEM((3 * inner, width), BF16),
            pltpu.VMEM((inner, width), BF16),
            pltpu.SemaphoreType.DMA((2,)),
        ],
        compiler_params=pltpu.CompilerParams(vmem_limit_bytes=40 * 2**20),
        cost_estimate=pl.CostEstimate(
            flops=2 * 10**9, bytes_accessed=12 * 10**6, transcendentals=200_000
        ),
        name="block",
    )(
        *map(
            in_hbm,
            (
                counts,
                segment_ids.reshape(1, rows),
                merged_position.reshape(1, rows // MERGE),
                ln_gain,
                merge_gain,
                merge_bias,
                qkv_weight.T,
                out_weight,
            ),
        ),
        *state,
        grads,
    )
    came_back = exchange(results[:n_in], "dp", ranks)
    merged = swap(results[n_in])
    if beside:
        halves = merged[:, :, token_width:].astype(F32)
        norm_grads = jnp.sum(halves[:, :4] + halves[:, 4:], axis=0)
        for bit in range(ranks.bit_length() - 1):
            norm_grads = spread(norm_grads, "dp", ranks, (1 << bit,))
            if bit == 0:
                norm_grads, came_back = lax.optimization_barrier((norm_grads, came_back))
        merged = merged[:, :, :token_width]
    else:
        norm_grads = lax.psum(results[-1], ("dp", "ctx"))
    patch_grad = pl.pallas_call(
        functools.partial(unpack_kernel, sizes, capacity),
        out_shape=jax.ShapeDtypeStruct((source_units, UNIT, width), BF16),
        in_specs=[smem] + [vmem] * n_in,
        out_specs=vmem,
        compiler_params=pltpu.CompilerParams(vmem_limit_bytes=8 * 2**20),
        cost_estimate=pl.CostEstimate(
            flops=UNPACK_FLOPS, bytes_accessed=10**6, transcendentals=0
        ),
        name="unpack",
    )(in_hbm(counts), in_hbm(came_back[0]), *came_back[1:])
    return (
        merged.reshape(owner_slots, token_width),
        patch_grad.reshape(source_units * UNIT, width),
        norm_grads,
    )


def solution(mesh):
    return jax.shard_map(
        functools.partial(per_device, (mesh.shape["dp"], mesh.shape["ctx"])),
        mesh=mesh,
        in_specs=(
            P(("dp", "ctx"), None),
            P("ctx", None),
            P(("dp", "ctx")),
            P(("dp", "ctx")),
            P(),
            P(),
            P(),
            P(),
            P(),
            P(),
            P(("dp", "ctx"), None),
        ),
        out_specs=(P(("dp", "ctx"), None), P(("dp", "ctx"), None), P()),
        check_vma=False,
    )
```

```python
import functools

import jax
import jax.numpy as jnp
from jax import lax
from jax.experimental import pallas as pl
from jax.experimental.pallas import tpu as pltpu
from jax.sharding import PartitionSpec as P

HEAD = 80
UNIT = 32
MERGE = 4
EPS = 1e-06
NEG = -1e30
LANES = 128
WIN = 256
F32 = jnp.float32
BF16 = jnp.bfloat16
FRONT_FLOPS = 12 * 10**9
HOLD_PARTS = 6
HOLD_FLOPS = 10**8
UNPACK_FLOPS = 10**10


def paired(size):
    return size <= 8 and size & (size - 1) == 0


def peer_of(index, slot, size):
    return index ^ slot if paired(size) else slot


def place(slot, size):
    return (slot, 0) if paired(size) else (0, slot)


def in_hbm(array):
    return pltpu.with_memory_space_constraint(array, pltpu.HBM)


def pieces(size, shape, dtype):
    if paired(size):
        return [pltpu.HBM((1, *shape), dtype)] + [
            jax.ShapeDtypeStruct((1, *shape), dtype)
        ] * (size - 1)
    return [jax.ShapeDtypeStruct((size, *shape), dtype)]


def exchange(arrays, axis, size):
    if paired(size):
        return [arrays[0]] + [
            lax.ppermute(arrays[slot], axis, [(i, i ^ slot) for i in range(size)])
            for slot in range(1, size)
        ]
    return [lax.all_to_all(arrays[0], axis, split_axis=0, concat_axis=0, tiled=True)]


def spread(terms, axis, size, slots):
    others = [
        lax.ppermute(terms, axis, [(i, i ^ slot) for i in range(size)]) for slot in slots
    ]
    for other in others:
        terms = terms + other
    return terms


def starts(counts, ranks):
    out = [jnp.int32(0)]
    for rank in range(ranks - 1):
        out.append(out[-1] + counts[rank])
    return out


def chosen(values, index):
    out = values[0]
    for i in range(1, len(values)):
        out = jnp.where(index == i, values[i], out)
    return out


def pack_blocks(sizes, capacity, slots, counts, source, *rest):
    ranks = sizes[0]
    outs, sems = rest[:-1], rest[-1]
    me = lax.axis_index("dp")
    first = chosen(starts(counts, ranks), me)
    copies = []
    for i, slot in enumerate(slots):
        array, entry = (i, 0) if paired(ranks) else (0, slot)
        lead = lax.rem(peer_of(me, slot, ranks) + 8 * ranks - first, ranks)
        for k in range(capacity):
            block = jnp.minimum(lead + k * ranks, source.shape[0] - 1)
            copies.append(
                pltpu.make_async_copy(
                    source.at[block], outs[array].at[entry, k], sems.at[i * capacity + k]
                )
            )
            copies[-1].start()
    for copy in copies:
        copy.wait()


def hold(far, near, sems):
    count = sems.shape[0]
    step = far.shape[0] // count
    spans = [slice(i * step, (i + 1) * step) for i in range(count)]
    copies = [
        pltpu.make_async_copy(far.at[span], near.at[span], sems.at[i])
        for i, span in enumerate(spans)
    ]
    for copy in copies:
        copy.start()
    for copy in copies:
        copy.wait()


def moments(values):
    average = jnp.mean(values, axis=-1, keepdims=True)
    centred = values - average
    inverse = lax.rsqrt(jnp.mean(centred * centred, axis=-1, keepdims=True) + EPS)
    return centred * inverse, inverse


def norm_back(scaled, normed, inverse):
    centre = jnp.mean(scaled, axis=-1, keepdims=True)
    slope = jnp.mean(scaled * normed, axis=-1, keepdims=True)
    return inverse * (scaled - centre - normed * slope)


def dot(a, b, ca=1, cb=0):
    return lax.dot_general(a, b, (((ca,), (cb,)), ((), ())), preferred_element_type=F32)


def iota(shape, dim):
    return lax.broadcasted_iota(jnp.int32, shape, dim)


def front_kernel(sizes, capacity, *refs):
    ranks = sizes[0]
    n_in = ranks if paired(ranks) else 1
    counts, ln_gain, ln_bias, wq = refs[:4]
    arrived, refs = refs[4 : 4 + n_in], refs[4 + n_in :]
    xs, normed_ref, inverse_ref, qs, ks, vs = refs
    rows, width = xs.shape
    units = rows // UNIT
    inner = wq.shape[0] // 3
    thirds = [slice(part * inner, (part + 1) * inner) for part in range(3)]
    me = lax.axis_index("dp")
    begin = starts(counts, ranks)
    for unit in range(units):
        wanted = unit * ranks + me
        sender = jnp.int32(0)
        for rank in range(1, ranks):
            sender = jnp.where(begin[rank] <= wanted, rank, sender)
        kth = (wanted - chosen(begin, sender)) // ranks
        span = slice(unit * UNIT, (unit + 1) * UNIT)
        if n_in == 1:
            xs[span, :] = arrived[0][sender, kth]
        else:
            slot = sender ^ me
            value = arrived[0][0, kth]
            for i in range(1, n_in):
                value = jnp.where(slot == i, arrived[i][0, kth], value)
            xs[span, :] = value
    normed, inverse = moments(xs[...].astype(F32))
    normed_ref[...] = normed
    inverse_ref[...] = jnp.broadcast_to(inverse, inverse_ref.shape)
    gain, bias = ln_gain[...].reshape(1, width), ln_bias[...].reshape(1, width)
    shifted = (normed * gain + bias).astype(BF16)
    for ref, part in ((qs, 0), (ks, 1), (vs, 2)):
        ref[:, inner:] = jnp.zeros((rows, ref.shape[1] - inner), BF16)
        ref[:, :inner] = dot(shifted, wq[thirds[part], :], 1, 1).astype(BF16)


def block_kernel(sizes, capacity, *refs):
    ranks, owners = sizes
    n_in = ranks if paired(ranks) else 1
    counts, labels, positions, *params, wq_far, wo_far = refs[:8]
    xs, normed_ref, inverse_ref, qs, ks, vs, grads = refs[8:15]
    refs = refs[15:]
    back, refs = refs[:n_in], refs[n_in:]
    windows, terms_out, ats, ps, dqs, dks, dvs, gs, ws, rows_out, terms, wq, wo, sems = refs
    rows, width = xs.shape
    ln_gain, merge_gain, merge_bias = (ref[...].reshape(1, width) for ref in params)
    units = rows // UNIT
    inner = wo.shape[0]
    heads = inner // HEAD
    scale = HEAD ** (-0.5)
    tokens = rows // MERGE
    load_out = pltpu.make_async_copy(wo_far, wo, sems.at[0])
    load_qkv = pltpu.make_async_copy(wq_far, wq, sems.at[1])
    load_out.start()
    load_qkv.start()
    pair = grads.shape[1]
    slots = owners * pair
    me, column = lax.axis_index("dp"), lax.axis_index("ctx")
    begin = starts(counts, ranks)
    normed_in, inverse_in = normed_ref[...], inverse_ref[:, :1]

    label = jnp.broadcast_to(labels[...].astype(F32), (rows, rows))
    joined = (label == label.T) & (
        iota((rows, rows), 0) // UNIT == iota((rows, rows), 1) // UNIT
    )
    own = iota((rows, tokens), 0) // MERGE == iota((rows, tokens), 1)
    place_of = positions[...] - column * slots
    spot = jnp.sum(jnp.where(own, place_of.astype(F32), 0.0), axis=1, keepdims=True)
    spot_row = jnp.broadcast_to(spot, (rows, LANES)).T[:1, :]
    spot = spot.astype(jnp.int32)
    spot_row = spot_row.astype(jnp.int32)

    def slot_place(index):
        local = index % slots
        return (local % pair) * owners + local // pair

    lane = iota((rows, MERGE * slots), 1)
    take = (
        (iota((rows, MERGE * slots), 0) % MERGE == lane // slots) & (slot_place(lane) == spot)
    ).astype(BF16)
    lead = iota((MERGE * slots, rows), 0)
    put = (
        (iota((MERGE * slots, rows), 1) % MERGE == lead // slots) & (slot_place(lead) == spot_row)
    ).astype(BF16)

    zero = jnp.zeros((rows, gs.shape[1] - inner), BF16)
    ats[...] = jnp.zeros_like(ats)
    dqs[...] = jnp.zeros_like(dqs)
    dks[...] = jnp.zeros_like(dks)
    dvs[...] = jnp.zeros_like(dvs)

    win_lane = iota((rows, WIN), 1)
    none = jnp.zeros((), BF16)

    def window(two):
        at = 2 * two * HEAD
        low = at // LANES * LANES
        first = (win_lane >= at - low) & (win_lane < at - low + HEAD)
        second = (win_lane >= at - low + HEAD) & (win_lane < at - low + 2 * HEAD)
        return slice(low, low + WIN), first, second

    def stacked(value, first, second):
        return jnp.concatenate(
            [jnp.where(first, value, none), jnp.where(second, value, none)], axis=0
        )

    def own_part(value, first, second):
        return jnp.where(first, value[:rows], jnp.where(second, value[rows:], 0.0))

    for two in range(heads // 2):
        span, first, second = window(two)
        scores = dot(qs[:, span], stacked(ks[:, span], first, second), 1, 1) * scale
        for side in range(2):
            half = slice(side * rows, (side + 1) * rows)
            score = jnp.where(joined, scores[:, half], NEG)
            raised = jnp.exp(score - jnp.max(score, axis=-1, keepdims=True))
            ps[two, :, half] = raised / jnp.sum(raised, axis=-1, keepdims=True)
        ats[:, span] += dot(ps[two].astype(BF16), stacked(vs[:, span], first, second))
    load_out.wait()
    hidden = xs[...].astype(F32) + dot(ats[:, :inner].astype(BF16), wo[...])
    normed_out, inverse_out = moments(hidden)
    result = (normed_out * merge_gain + merge_bias).astype(BF16)
    ws[...] = dot(put, result)
    for owner in range(owners):
        for part in range(MERGE):
            start = part * slots + owner * pair
            windows[owner, :, part * width : (part + 1) * width] = ws[
                start : start + pair, :
            ].astype(BF16)

    for owner in range(owners):
        for part in range(MERGE):
            start = part * slots + owner * pair
            ws[start : start + pair, :] = grads[
                owner, :, part * width : (part + 1) * width
            ].astype(F32)
    upstream = dot(take, ws[...].astype(BF16))
    terms[2:3, :] = jnp.sum(upstream * normed_out, axis=0, keepdims=True)
    terms[3:4, :] = jnp.sum(upstream, axis=0, keepdims=True)
    hidden_grad = norm_back(upstream * merge_gain, normed_out, inverse_out)
    gs[:, :inner] = dot(hidden_grad.astype(BF16), wo[...], 1, 1).astype(BF16)
    gs[:, inner:] = zero
    for two in range(heads // 2):
        span, first, second = window(two)
        prob = ps[two]
        grad = gs[:, span]
        prob_grad = dot(grad, stacked(vs[:, span], first, second), 1, 1)
        dvs[:, span] += own_part(dot(prob.astype(BF16), grad, 0, 0), first, second)
        weighted = prob * prob_grad
        centred = [
            prob_grad[:, half] - jnp.sum(weighted[:, half], axis=-1, keepdims=True)
            for half in (slice(0, rows), slice(rows, 2 * rows))
        ]
        score_grad = (prob * jnp.concatenate(centred, axis=1) * scale).astype(BF16)
        dqs[:, span] += dot(score_grad, stacked(ks[:, span], first, second))
        dks[:, span] += own_part(dot(score_grad, qs[:, span], 0, 0), first, second)
    load_qkv.wait()
    input_grad = sum(
        dot(ref[:, :inner].astype(BF16), wq[part * inner : (part + 1) * inner, :])
        for ref, part in ((dqs, 0), (dks, 1), (dvs, 2))
    )
    terms[0:1, :] = jnp.sum(input_grad * normed_in, axis=0, keepdims=True)
    terms[1:2, :] = jnp.sum(input_grad, axis=0, keepdims=True)
    row_grad = hidden_grad + norm_back(input_grad * ln_gain, normed_in, inverse_in)
    rows_out[...] = row_grad.astype(BF16).reshape(units, UNIT, width)

    terms_out[...] = terms[...]
    spare = windows.shape[2] - MERGE * width
    if spare:
        high = terms[...].astype(BF16)
        low = (terms[...] - high.astype(F32)).astype(BF16)
        for owner in range(owners):
            windows[owner, :, MERGE * width :] = jnp.concatenate([high, low], axis=0)

    for slot in range(ranks):
        array, entry = place(slot, ranks)
        peer = peer_of(me, slot, ranks)
        base_of = chosen(begin, peer)
        low = lax.rem(me + 8 * ranks - base_of, ranks)
        for k in range(capacity):
            unit = jnp.minimum((base_of + low + k * ranks) // ranks, units - 1)
            back[array][entry, k] = rows_out[unit]


def unpack_kernel(sizes, capacity, *refs):
    ranks = sizes[0]
    counts, *came, patch_grad = refs
    me = lax.axis_index("dp")
    first = chosen(starts(counts, ranks), me)
    live = chosen([counts[rank] for rank in range(ranks)], me)
    for slot in range(ranks):
        array, entry = place(slot, ranks)
        low = lax.rem(peer_of(me, slot, ranks) + 8 * ranks - first, ranks)
        for k in range(capacity):
            block = low + k * ranks

            @pl.when(block < live)
            def _(array=array, entry=entry, k=k, block=block):
                patch_grad[block] = came[array][entry, k]

            @pl.when((block >= live) & (block < patch_grad.shape[0]))
            def _(block=block):
                patch_grad[block] = jnp.zeros(patch_grad.shape[1:], BF16)


def per_device(
    sizes,
    patches,
    unit_counts,
    segment_ids,
    merged_position,
    ln_gain,
    ln_bias,
    qkv_weight,
    out_weight,
    merge_gain,
    merge_bias,
    merged_grad,
):
    ranks, owners = sizes
    width = patches.shape[1]
    source_units = patches.shape[0] // UNIT
    rows = segment_ids.shape[0]
    capacity = -(-source_units // ranks)
    owner_slots, token_width = merged_grad.shape
    pair = owner_slots // owners
    inner = out_weight.shape[0]
    heads = inner // HEAD
    padded = -(-inner // LANES) * LANES
    counts = unit_counts.reshape(-1)
    smem = pl.BlockSpec(memory_space=pltpu.SMEM)
    vmem = pl.BlockSpec(memory_space=pltpu.VMEM)
    anywhere = pl.BlockSpec(memory_space=pl.ANY)

    block_shapes = pieces(ranks, (capacity, UNIT, width), BF16)
    beside = paired(ranks) and paired(owners) and pair == 8
    window_shape = jax.ShapeDtypeStruct(
        (owners, pair, token_width + (width if beside else 0)), BF16
    )
    n_in = len(block_shapes)
    swap = functools.partial(
        lax.all_to_all, axis_name="ctx", split_axis=0, concat_axis=0, tiled=True
    )

    def packed(slots, shapes, name):
        return pl.pallas_call(
            functools.partial(pack_blocks, sizes, capacity, slots),
            out_shape=shapes,
            in_specs=[smem, anywhere],
            out_specs=[vmem] * len(shapes),
            scratch_shapes=[pltpu.SemaphoreType.DMA((len(slots) * capacity,))],
            compiler_params=pltpu.CompilerParams(vmem_limit_bytes=4 * 2**20),
            name=name,
        )(in_hbm(counts), in_hbm(patches.reshape(source_units, UNIT, width)))

    if paired(ranks):
        outgoing = [
            *packed([0], block_shapes[:1], "pack_own"),
            *packed(range(1, ranks), block_shapes[1:], "pack_blocks"),
        ]
    else:
        outgoing = packed(range(ranks), block_shapes, "pack_blocks")
    arrived = exchange(outgoing, "dp", ranks)

    grad_blocks = merged_grad.reshape(owners, pair, token_width)
    grads = swap(grad_blocks)

    near = pl.pallas_call(
        hold,
        out_shape=pltpu.VMEM(qkv_weight.T.shape, BF16),
        in_specs=[anywhere],
        out_specs=vmem,
        scratch_shapes=[pltpu.SemaphoreType.DMA((HOLD_PARTS,))],
        compiler_params=pltpu.CompilerParams(vmem_limit_bytes=2**20),
        cost_estimate=pl.CostEstimate(flops=HOLD_FLOPS, bytes_accessed=10**6, transcendentals=0),
        name="hold",
    )(in_hbm(qkv_weight.T))

    wide = jax.ShapeDtypeStruct((rows, padded), BF16)
    state = pl.pallas_call(
        functools.partial(front_kernel, sizes, capacity),
        out_shape=[
            jax.ShapeDtypeStruct((rows, width), BF16),
            jax.ShapeDtypeStruct((rows, width), F32),
            jax.ShapeDtypeStruct((rows, LANES), F32),
            wide,
            wide,
            wide,
        ],
        in_specs=[smem] + [vmem] * (3 + n_in),
        out_specs=[vmem] * 6,
        compiler_params=pltpu.CompilerParams(vmem_limit_bytes=16 * 2**20),
        cost_estimate=pl.CostEstimate(
            flops=FRONT_FLOPS, bytes_accessed=8 * 10**6, transcendentals=0
        ),
        name="front",
    )(
        *map(in_hbm, (counts, ln_gain, ln_bias)),
        near,
        in_hbm(arrived[0]),
        *arrived[1:],
    )

    results = pl.pallas_call(
        functools.partial(block_kernel, sizes, capacity),
        out_shape=[
            *(jax.ShapeDtypeStruct(shape.shape, BF16) for shape in block_shapes),
            window_shape,
            jax.ShapeDtypeStruct((4, width), F32),
        ],
        in_specs=[smem] + [vmem] * 5 + [anywhere] * 2 + [vmem] * 7,
        out_specs=[vmem] * (n_in + 2),
        scratch_shapes=[
            pltpu.VMEM((rows, padded), F32),
            pltpu.VMEM((heads // 2, rows, 2 * rows), F32),
            pltpu.VMEM((rows, padded), F32),
            pltpu.VMEM((rows, padded), F32),
            pltpu.VMEM((rows, padded), F32),
            pltpu.VMEM((rows, padded), BF16),
            pltpu.VMEM((MERGE * owners * pair, width), F32),
            pltpu.VMEM((rows // UNIT, UNIT, width), BF16),
            pltpu.VMEM((4, width), F32),
            pltpu.VMEM((3 * inner, width), BF16),
            pltpu.VMEM((inner, width), BF16),
            pltpu.SemaphoreType.DMA((2,)),
        ],
        compiler_params=pltpu.CompilerParams(vmem_limit_bytes=40 * 2**20),
        cost_estimate=pl.CostEstimate(
            flops=2 * 10**9, bytes_accessed=12 * 10**6, transcendentals=200_000
        ),
        name="block",
    )(
        *map(
            in_hbm,
            (
                counts,
                segment_ids.reshape(1, rows),
                merged_position.reshape(1, rows // MERGE),
                ln_gain,
                merge_gain,
                merge_bias,
                qkv_weight.T,
                out_weight,
            ),
        ),
        *state,
        grads,
    )
    came_back = exchange(results[:n_in], "dp", ranks)
    merged = swap(results[n_in])
    if beside:
        halves = merged[:, :, token_width:].astype(F32)
        norm_grads = jnp.sum(halves[:, :4] + halves[:, 4:], axis=0)
        for bit in range(ranks.bit_length() - 1):
            norm_grads = spread(norm_grads, "dp", ranks, (1 << bit,))
            if bit == 0:
                norm_grads, came_back = lax.optimization_barrier((norm_grads, came_back))
        merged = merged[:, :, :token_width]
    else:
        norm_grads = lax.psum(results[-1], ("dp", "ctx"))
    patch_grad = pl.pallas_call(
        functools.partial(unpack_kernel, sizes, capacity),
        out_shape=jax.ShapeDtypeStruct((source_units, UNIT, width), BF16),
        in_specs=[smem] + [vmem] * n_in,
        out_specs=vmem,
        compiler_params=pltpu.CompilerParams(vmem_limit_bytes=8 * 2**20),
        cost_estimate=pl.CostEstimate(
            flops=UNPACK_FLOPS, bytes_accessed=10**6, transcendentals=0
        ),
        name="unpack",
    )(in_hbm(counts), *came_back)
    return (
        merged.reshape(owner_slots, token_width),
        patch_grad.reshape(source_units * UNIT, width),
        norm_grads,
    )


def solution(mesh):
    return jax.shard_map(
        functools.partial(per_device, (mesh.shape["dp"], mesh.shape["ctx"])),
        mesh=mesh,
        in_specs=(
            P(("dp", "ctx"), None),
            P("ctx", None),
            P(("dp", "ctx")),
            P(("dp", "ctx")),
            P(),
            P(),
            P(),
            P(),
            P(),
            P(),
            P(("dp", "ctx"), None),
        ),
        out_specs=(P(("dp", "ctx"), None), P(("dp", "ctx"), None), P()),
        check_vma=False,
    )
```
